256 devices in a mesh: clip: 16 (over x, y_lo, core), copy: 16 (over z, y_hi).
Axes of the slice: x: 4, y: 4 (y_hi: 2, y_lo: 2; y = y_hi * 2 + y_lo), z: 8, core: 2. Of those that a mesh axis runs over, the one named last changes fastest.
Arguments:
- frames: bfloat16 [16, 256, 1024], P('clip', 'copy'), may hold values from -6 to 6
- targets: bfloat16 [16, 256, 1024], P('clip', 'copy'), may hold values from -6 to 6
- kept_index: int32 [16, 16, 128], P('clip', 'copy'), may hold values from 0 to 255, as said below
- kept_count: int32 [16, 16], P('clip', 'copy'), may hold values from 64 to 128, as said below
- fill_slot: int32 [16, 16, 256], P('clip', 'copy'), may hold values from 0 to 128, as said below
- norm_gain: float32 [1024], replicated, may hold values from 0.5 to 1.5
- w_qkv: bfloat16 [1024, 3072], P('clip'), may hold values from -8 to 8
- w_out: bfloat16 [1024, 1024], P('clip'), may hold values from -0.1875 to 0.1875
- mask_embed: bfloat16 [1024], replicated, may hold values from -4 to 4
- dec_kernel: float32 [7, 1024], replicated, may hold values from -2 to 2
Outputs:
- encoded: bfloat16 [16, 16, 128, 1024], P('clip', 'copy')
- grad_qkv: float32 [1024, 3072], P('clip', 'copy')
- grad_out: float32 [1024, 1024], P('clip', 'copy')
The draws below stay inside these ranges and needn't reach their ends.
Inputs may be any that keep to these rules, and one draw needn't show every extreme that they name: `kept_count`: some copy of every clip keeps exactly 128 frames. `kept_index`: for each copy the first kept_count entries are the kept frame positions in rising order, the rest are other frames of the clip in rising order; no position repeats. `fill_slot`: a kept frame holds its row among the first kept_count entries of kept_index, every other frame holds 128.
All inputs are finite; a program needn't handle non-finite values.
Results may differ from the reference program's by a relative error of at most 0.017.
Values may be sent and summed in bfloat16 or wider, within the bound.
No kernel may reach another device: no remote copies, remote signals or barrier semaphores. Data moves between devices by JAX's collectives and lax.ppermute only.
A program may use at most 64 MiB of HBM per device.

```python
import jax
import jax.numpy as jnp
from jax import lax

D = 1024
H = 16
HS = 64
HW = 1024
L = 256
KMAX = 128
KW = 7
CLIPS = 16
COPIES = 16


def mask_plan(key):
    count_key, pick_key, ordering_key = jax.random.split(key, 3)
    counts = jax.random.randint(count_key, (CLIPS, COPIES), L // 4, KMAX + 1)
    fullest = jax.random.randint(pick_key, (CLIPS, 1), 0, COPIES)
    counts = jnp.where(jnp.arange(COPIES)[None, :] == fullest, KMAX, counts).astype(jnp.int32)
    item_keys = jax.random.split(ordering_key, CLIPS * COPIES)
    ranking = jax.vmap(lambda item_key: jax.random.permutation(item_key, L))(item_keys).reshape(CLIPS, COPIES, L)
    kept_mask = ranking < counts[:, :, None]
    places = jnp.arange(L, dtype=jnp.int32)
    ordering = jnp.argsort(jnp.where(kept_mask, places, places + L), axis=-1)
    kept_rows = ordering[:, :, :KMAX].astype(jnp.int32)
    slot_map = jnp.where(kept_mask, jnp.cumsum(kept_mask.astype(jnp.int32), axis=-1) - 1, KMAX).astype(jnp.int32)
    return (kept_rows, counts, slot_map)


def draw_kept_index(key, part):
    return mask_plan(key)[0]


def draw_kept_count(key, part):
    return mask_plan(key)[1]


def draw_fill_slot(key, part):
    return mask_plan(key)[2]


def draw_w_qkv(key, part):
    key = jax.random.fold_in(key, 7)
    limit = 6.0 * D ** (-0.5)
    base = jnp.clip(jax.random.normal(key, (D, 3 * HW), jnp.float32) * D ** (-0.5), -limit, limit)
    return base.astype(jnp.bfloat16)


def block_levels(stream_key, shape, shards, least, high):
    level = 1.0
    for dim, shards_of in shards:
        steps = jax.random.uniform(jax.random.fold_in(jax.random.fold_in(stream_key, 6), dim), (shards_of,), jnp.float32, least / len(shards), high / len(shards))
        level = level * jnp.repeat(jnp.exp(steps), shape[dim] // shards_of).reshape((-1,) + (1,) * (len(shape) - 1 - dim))
    return level


def noise(stream_key, dims, width, bound, pieces=(), kind=jnp.bfloat16):
    result = jax.random.normal(stream_key, dims, jnp.float32) * width
    if len(pieces) > 0:
        result = block_levels(stream_key, dims, pieces, -0.22, 0.18) * result
    return jnp.clip(result, min=-bound, max=bound).astype(kind)


def setup_inputs(seed: int = 0) -> dict:
    seeds = jax.random.split(jax.random.key(seed), 11)
    return {
        "frames": noise(seeds[0], (CLIPS, L, D), 1.0, 6.0, ((0, 16), (1, 16))),
        "targets": noise(seeds[1], (CLIPS, L, D), 1.0, 6.0, ((0, 16), (1, 16))),
        "kept_index": draw_kept_index(jax.random.fold_in(seeds[10], 71), 0),
        "kept_count": draw_kept_count(jax.random.fold_in(seeds[10], 71), 0),
        "fill_slot": draw_fill_slot(jax.random.fold_in(seeds[10], 71), 0),
        "norm_gain": jnp.clip(jax.random.uniform(seeds[5], (D,), jnp.float32, 0.5, 1.5), 0.5, 1.5),
        "w_qkv": draw_w_qkv(jax.random.fold_in(seeds[10], 71), 0),
        "w_out": noise(seeds[7], (HW, D), HW ** -0.5, 0.1875, ((0, 16),)),
        "mask_embed": noise(seeds[8], (D,), 1.0, 4.0),
        "dec_kernel": noise(seeds[9], (KW, D), 0.4, 2.0, (), jnp.float32),
    }


NORM_EPSILON = 1e-05
MASKED_SCORE = -1e+30

def layer_norm_rows(row_block, norm_gain):
    values = row_block.astype(jnp.float32)
    center = values - lax.optimization_barrier(jnp.mean(values, axis=1, keepdims=True))
    spread = lax.optimization_barrier(jnp.mean(center * center, axis=1, keepdims=True))
    return (center * lax.rsqrt(spread + NORM_EPSILON) * norm_gain[None, :]).astype(jnp.bfloat16)

def depthwise(field, dec_kernel, flipped):
    reach = dec_kernel.shape[0] // 2
    length = field.shape[0]
    padded = jnp.pad(field, ((reach, reach), (0, 0)))
    total = jnp.zeros_like(field)
    for tap_index in range(dec_kernel.shape[0]):
        begin = 2 * reach - tap_index if flipped else tap_index
        total = total + dec_kernel[tap_index][None, :] * padded[begin:begin + length]
    return total

def softmax_probs(queries, keys_part, live_keys, score_scale):
    scores = jnp.einsum('qhd,khd->hqk', queries.astype(jnp.float32), keys_part.astype(jnp.float32)) * score_scale
    scores = jnp.where(live_keys[None, None, :], scores, MASKED_SCORE)
    highest = lax.optimization_barrier(jnp.max(scores, axis=-1, keepdims=True))
    raised = jnp.exp(scores - highest)
    return raised / lax.optimization_barrier(jnp.sum(raised, axis=-1, keepdims=True))

def copy_step(clip_frames, clip_targets, positions, kept_total, slot_map, norm_gain, w_qkv, w_out, mask_embed, dec_kernel):
    score_scale = HS ** (-0.5)
    loss_scale = (KMAX * CLIPS * COPIES) ** (-0.5)
    live_keys = jnp.arange(KMAX) < kept_total
    inputs = jnp.take(clip_frames, positions, axis=0)
    normed = layer_norm_rows(inputs, norm_gain)
    projected = jnp.dot(normed, w_qkv, preferred_element_type=jnp.float32).astype(jnp.bfloat16)
    queries = projected[:, :HW].reshape(KMAX, H, HS)
    keys_part = projected[:, HW:2 * HW].reshape(KMAX, H, HS)
    values = projected[:, 2 * HW:].reshape(KMAX, H, HS)
    probs = softmax_probs(queries, keys_part, live_keys, score_scale)
    probs_low = probs.astype(jnp.bfloat16)
    context = jnp.einsum('hqk,khd->qhd', probs_low.astype(jnp.float32), values.astype(jnp.float32))
    context = context.astype(jnp.bfloat16).reshape(KMAX, HW)
    mixed = inputs.astype(jnp.float32) + jnp.dot(context, w_out, preferred_element_type=jnp.float32)
    encoded = jnp.where(live_keys[:, None], mixed, 0.0).astype(jnp.bfloat16)
    table = jnp.concatenate([encoded, mask_embed[None, :]], axis=0)
    filled = jnp.take(table, slot_map, axis=0)
    predicted = depthwise(filled.astype(jnp.float32), dec_kernel, False)
    masked_frames = slot_map == KMAX
    error = jnp.where(masked_frames[:, None], predicted - clip_targets.astype(jnp.float32), 0.0) * loss_scale
    dfilled = depthwise(error, dec_kernel, True)
    dencoded = jnp.where(live_keys[:, None], jnp.take(dfilled, positions, axis=0), 0.0).astype(jnp.bfloat16)
    out_term = jnp.dot(context.T, dencoded, preferred_element_type=jnp.float32)
    dcontext = jnp.dot(dencoded, w_out.T, preferred_element_type=jnp.float32).astype(jnp.bfloat16)
    dcontext = dcontext.reshape(KMAX, H, HS).astype(jnp.float32)
    dprobs = jnp.einsum('qhd,khd->hqk', dcontext, values.astype(jnp.float32))
    dvalues = jnp.einsum('hqk,qhd->khd', probs_low.astype(jnp.float32), dcontext)
    dscores = probs * (dprobs - lax.optimization_barrier(jnp.sum(probs * dprobs, axis=-1, keepdims=True))) * score_scale
    dscores = dscores.astype(jnp.bfloat16).astype(jnp.float32)
    dqueries = jnp.einsum('hqk,khd->qhd', dscores, keys_part.astype(jnp.float32))
    dkeys = jnp.einsum('hqk,qhd->khd', dscores, queries.astype(jnp.float32))
    dprojected = jnp.concatenate([dqueries.reshape(KMAX, HW), dkeys.reshape(KMAX, HW), dvalues.reshape(KMAX, HW)], axis=1).astype(jnp.bfloat16)
    qkv_term = jnp.dot(normed.T, dprojected, preferred_element_type=jnp.float32)
    return (encoded, qkv_term, out_term)

def reference(frames, targets, kept_index, kept_count, fill_slot, norm_gain, w_qkv, w_out, mask_embed, dec_kernel):

    def clip_step(carry, clip_items):
        clip_frames, clip_targets, index_rows, count_row, slot_rows = clip_items

        def copy_loop(inner_carry, copy_items):
            positions, kept_total, slot_map = copy_items
            encoded, qkv_term, out_term = copy_step(clip_frames, clip_targets, positions, kept_total, slot_map, norm_gain, w_qkv, w_out, mask_embed, dec_kernel)
            return ((inner_carry[0] + qkv_term, inner_carry[1] + out_term), encoded)
        return lax.scan(copy_loop, carry, (index_rows, count_row, slot_rows))
    initial = (jnp.zeros((D, 3 * HW), jnp.float32), jnp.zeros((HW, D), jnp.float32))
    totals, encoded = lax.scan(clip_step, initial, (frames, targets, kept_index, kept_count, fill_slot))
    return (encoded, totals[0], totals[1])
```

```python
import jax
import jax.numpy as jnp
from jax import lax
from jax.experimental import pallas as pl
from jax.experimental.pallas import tpu as pltpu
from jax.sharding import Mesh
from jax.sharding import PartitionSpec as P


D = 1024
H = 16
HS = 64
L = 256
KMAX = 128
KW = 7
CLIPS = 16
COPIES = 16
QALL = COPIES * KMAX
NORM_EPSILON = 1e-05
MASKED_SCORE = -1e30
SCORE_SCALE = HS**-0.5
LOSS_SCALE = (KMAX * CLIPS * COPIES) ** -0.5
PAD = 8
LANES = 256
VMEM_LIMIT = 48 * 1024 * 1024

CLIP = ("x", "y_lo", "core")
COPY = ("z", "y_hi")
F32 = jnp.float32
BF16 = jnp.bfloat16


def mm(left, right):
    return jnp.dot(left, right, preferred_element_type=F32)


def mm_nt(left, right):
    return lax.dot_general(left, right, (((1,), (1,)), ((), ())), preferred_element_type=F32)


def whole(count):
    return [pl.BlockSpec(memory_space=pltpu.VMEM)] * count


def params():
    return pltpu.CompilerParams(vmem_limit_bytes=VMEM_LIMIT)


def forward_kernel(
    got_ref, w_ref, gain_ref, ctx_ref, probs_ref, pick_ref, query_ref, key_ref, value_ref, normed_ref, wv_ref
):
    values = got_ref[:, :D].astype(F32)
    center = values - jnp.mean(values, axis=1, keepdims=True)
    spread = jnp.mean(center * center, axis=1, keepdims=True)
    normed = (center * lax.rsqrt(spread + NORM_EPSILON) * gain_ref[...]).astype(BF16)
    normed_ref[...] = normed.T
    for c in range(CLIPS):
        wv_ref[c * HS : c * HS + HS // 2, :] = w_ref[c, HS:, :HS]
        wv_ref[c * HS + HS // 2 : (c + 1) * HS, :] = w_ref[c, HS:, HS:]
    qk = mm(normed, w_ref[:, :HS, :].reshape(D, 2 * HS)).astype(BF16)
    v = mm(normed, wv_ref[...]).astype(BF16)
    qk_t = qk.astype(F32).T
    query_t = (qk_t[:HS] * SCORE_SCALE).astype(BF16)
    key = qk[:, HS:]
    key_ref[...] = qk_t[HS:].astype(BF16)
    value_ref[...] = v
    value_t = v.astype(F32).T.astype(BF16)
    rows = lax.broadcasted_iota(jnp.int32, (L, KMAX), 0).astype(F32)
    for m in range(COPIES):
        lanes = slice(m * KMAX, (m + 1) * KMAX)
        index = got_ref[m * 16 : (m + 1) * 16, D:].astype(F32)[:1]
        hit = jnp.where(rows == index, 1.0, 0.0)
        pick = hit.astype(BF16)
        pick_ref[:, lanes] = pick
        queries = mm(query_t, pick).astype(BF16)
        query_ref[:, lanes] = queries
        kept = jnp.sum(hit, axis=1, keepdims=True)
        scores = jnp.where(kept > 0.5, mm(key, queries), MASKED_SCORE)
        raised = jnp.exp(scores - jnp.max(scores, axis=0, keepdims=True))
        probs = raised / jnp.sum(raised, axis=0, keepdims=True)
        probs_ref[:, lanes] = probs
        ctx_ref[m] = mm(value_t, probs.astype(BF16)).astype(BF16)


def forward(got, weights, gain):
    return pl.pallas_call(
        forward_kernel,
        out_shape=[
            jax.ShapeDtypeStruct((COPIES, HS, KMAX), BF16),
            jax.ShapeDtypeStruct((L, QALL), F32),
            jax.ShapeDtypeStruct((L, QALL), BF16),
            jax.ShapeDtypeStruct((HS, QALL), BF16),
            jax.ShapeDtypeStruct((HS, L), BF16),
            jax.ShapeDtypeStruct((L, HS), BF16),
            jax.ShapeDtypeStruct((D, L), BF16),
        ],
        in_specs=whole(3),
        out_specs=whole(7),
        scratch_shapes=[pltpu.VMEM((D, HS), BF16)],
        compiler_params=params(),
        name="forward",
    )(got, weights, gain)


def decoder_kernel(
    count_ref, ctx_ref, got_ref, w_ref, targets_ref, index_ref, embed_ref, taps_ref, encoded_ref, dctx_ref, denc_ref, field_ref
):
    live = lax.broadcasted_iota(jnp.int32, (KMAX, 1), 0) < count_ref[0]
    rows = lax.broadcasted_iota(jnp.int32, (L, KMAX), 0).astype(F32)
    hit = jnp.where(rows == index_ref[:1].astype(F32), 1.0, 0.0)
    masked = 1.0 - jnp.sum(hit, axis=1, keepdims=True)
    place = hit.astype(BF16)
    pick = hit.T.astype(BF16)
    ctx = ctx_ref[...].T
    reach = KW // 2
    field_ref[:PAD] = jnp.zeros((PAD, LANES), F32)
    field_ref[PAD + L :] = jnp.zeros((PAD, LANES), F32)
    for c in range(D // LANES):
        lanes = slice(c * LANES, (c + 1) * LANES)
        mixed = mm(pick, got_ref[:, lanes]) + mm(ctx, w_ref[:, lanes])
        encoded = jnp.where(live, mixed, 0.0).astype(BF16)
        encoded_ref[:, lanes] = encoded
        field_ref[PAD : PAD + L] = mm(place, encoded) + masked * embed_ref[:, lanes].astype(F32)
        predicted = taps_ref[:1, lanes] * field_ref[PAD - reach : PAD - reach + L]
        for t in range(1, KW):
            begin = PAD - reach + t
            predicted = predicted + taps_ref[t : t + 1, lanes] * field_ref[begin : begin + L]
        error = masked * (predicted - targets_ref[:, lanes].astype(F32)) * LOSS_SCALE
        field_ref[PAD : PAD + L] = error
        dfilled = taps_ref[:1, lanes] * field_ref[PAD + reach : PAD + reach + L]
        for t in range(1, KW):
            begin = PAD + reach - t
            dfilled = dfilled + taps_ref[t : t + 1, lanes] * field_ref[begin : begin + L]
        denc_ref[:, lanes] = mm(pick, dfilled.astype(BF16)).astype(BF16)
    dctx_ref[...] = mm_nt(w_ref[...], denc_ref[...]).astype(BF16)


def decoder(count, ctx, got, w_out, targets, index, embed, taps):
    return pl.pallas_call(
        decoder_kernel,
        out_shape=[
            jax.ShapeDtypeStruct((KMAX, D), BF16),
            jax.ShapeDtypeStruct((D, KMAX), BF16),
            jax.ShapeDtypeStruct((KMAX, D), BF16),
        ],
        in_specs=[pl.BlockSpec(memory_space=pltpu.SMEM)] + whole(7),
        out_specs=whole(3),
        scratch_shapes=[pltpu.VMEM((L + 2 * PAD, LANES), F32)],
        compiler_params=params(),
        name="decoder",
    )(count, ctx, got, w_out, targets, index, embed, taps)


def out_grad_kernel(core_ref, ctx_ref, denc_ref, out_ref):
    half_rows = HS // 2
    for c in range(CLIPS):
        half = jnp.where(core_ref[0] == c % 2, 0, 1)
        block = mm(ctx_ref[c * HS : (c + 1) * HS, :], denc_ref[...])
        upper, lower = block[:half_rows], block[half_rows:]
        for a in range(D // 128):
            lanes = slice(a * 128, (a + 1) * 128)
            first, second = upper[:, lanes], lower[:, lanes]
            even = jnp.concatenate([first[:, :HS], second[:, :HS]], axis=1)
            odd = jnp.concatenate([first[:, HS:], second[:, HS:]], axis=1)
            out_ref[half, c // 2, 2 * a] = even.astype(BF16)
            out_ref[half, c // 2, 2 * a + 1] = odd.astype(BF16)


def out_grad(core, ctx, denc):
    return pl.pallas_call(
        out_grad_kernel,
        out_shape=jax.ShapeDtypeStruct((2, CLIPS // 2, COPIES, HS // 2, 2 * HS), BF16),
        in_specs=[pl.BlockSpec(memory_space=pltpu.SMEM)] + whole(2),
        out_specs=pl.BlockSpec(memory_space=pltpu.VMEM),
        compiler_params=params(),
        name="out_grad",
    )(core, ctx, denc)


def backward_kernel(
    dctx_ref, probs_ref, pick_ref, query_ref, key_ref, value_ref, normed_ref, out_ref, dctx_all, low_all, ds_all, dq_all
):
    key_t = key_ref[...]
    value = value_ref[...]
    for m in range(COPIES):
        lanes = slice(m * KMAX, (m + 1) * KMAX)
        dctx = dctx_ref[m]
        dctx_all[:, lanes] = dctx
        probs = probs_ref[:, lanes]
        low_all[:, lanes] = probs.astype(BF16)
        dprobs = mm(value, dctx)
        dscores = probs * (dprobs - jnp.sum(probs * dprobs, axis=0, keepdims=True))
        dscores = dscores.astype(BF16)
        ds_all[:, lanes] = dscores
        dq_all[:, lanes] = (mm(key_t, dscores) * SCORE_SCALE).astype(BF16)
    dvalue = mm_nt(dctx_all[...], low_all[...]).astype(BF16)
    dkey = mm_nt(query_ref[...], ds_all[...]).astype(BF16)
    dquery = mm_nt(dq_all[...], pick_ref[...]).astype(BF16)
    normed_t = normed_ref[...]
    grad_qk = mm_nt(normed_t, jnp.concatenate([dquery, dkey], axis=0)).astype(BF16)
    grad_v = mm_nt(normed_t, dvalue).astype(BF16)
    for c in range(CLIPS):
        out_ref[c, :HS, :] = grad_qk[c * HS : (c + 1) * HS]
        out_ref[c, HS:, :HS] = grad_v[c * HS : c * HS + HS // 2]
        out_ref[c, HS:, HS:] = grad_v[c * HS + HS // 2 : (c + 1) * HS]


def backward(dctx, probs, pick, query, key, value, normed):
    return pl.pallas_call(
        backward_kernel,
        out_shape=jax.ShapeDtypeStruct((CLIPS, HS + HS // 2, 2 * HS), BF16),
        in_specs=whole(7),
        out_specs=pl.BlockSpec(memory_space=pltpu.VMEM),
        scratch_shapes=[
            pltpu.VMEM((HS, QALL), BF16),
            pltpu.VMEM((L, QALL), BF16),
            pltpu.VMEM((L, QALL), BF16),
            pltpu.VMEM((HS, QALL), BF16),
        ],
        compiler_params=params(),
        name="backward",
    )(dctx, probs, pick, query, key, value, normed)


def swap(array, axes):
    return lax.all_to_all(array, axes, 0, 0, tiled=True)


def side_by_side(block):
    half = block.shape[0] // 2
    return jnp.concatenate([block[:half], block[half:]], axis=1)


def stacked(block):
    half = block.shape[-1] // 2
    return jnp.concatenate([block[..., :half], block[..., half:]], axis=-2)


def per_device(
    frames,
    targets,
    kept_index,
    kept_count,
    fill_slot,
    norm_gain,
    w_qkv,
    w_out,
    mask_embed,
    dec_kernel,
):
    copy_at = lax.axis_index(COPY)
    core = lax.axis_index("core")
    count = kept_count[0]
    live = jnp.arange(KMAX)[None, :] < count[0]
    index = jnp.broadcast_to(jnp.where(live, kept_index[0], L).astype(BF16), (16, KMAX))

    packed = jnp.concatenate([frames[0], index], axis=1)
    got = swap(jnp.broadcast_to(packed[None], (COPIES,) + packed.shape), COPY).reshape(L, D + KMAX)

    wq, wk, wv = [
        lax.dynamic_slice(w_qkv, (0, part * D + copy_at * HS), (HS, HS)) for part in range(3)
    ]
    weights = jnp.concatenate([jnp.concatenate([wq, wk], axis=1), side_by_side(wv)], axis=0)
    weights = lax.all_gather(weights, CLIP, axis=0)
    w_out_all = lax.all_gather(w_out, CLIP, axis=0, tiled=True)
    targets_all = lax.all_gather(lax.all_gather(targets[0], "y_hi", axis=0), "z", axis=0)
    targets_all = targets_all.reshape(L, D)

    ctx, probs, pick, query, key, value, normed = forward(got, weights, norm_gain[None, :])
    ctx = swap(ctx, COPY).reshape(D, KMAX)
    encoded, dctx, denc = decoder(
        count, ctx, got, w_out_all, targets_all, index, mask_embed[None, :], dec_kernel
    )
    dctx = swap(dctx.reshape(H, HS, KMAX), COPY)

    out_term = out_grad(core.reshape(1), ctx, denc)
    other = lax.ppermute(out_term[1], "core", [(0, 1), (1, 0)])
    out_term = (out_term[0].astype(F32) + other.astype(F32)).astype(BF16)
    out_term = swap(out_term, ("x", "y_lo"))
    out_term = jnp.sum(out_term.astype(F32), axis=0).astype(BF16)

    term = swap(backward(dctx, probs, pick, query, key, value, normed), CLIP)
    term = jnp.sum(term.astype(F32), axis=0).astype(BF16)
    to = jnp.arange(COPIES)[:, None, None]
    zero = jnp.zeros((HS // 2, 2 * HS), BF16)
    pieces = (side_by_side(term[:HS, :HS]), side_by_side(term[:HS, HS:]), term[HS:])
    sent = zero[None]
    for part, piece in enumerate(pieces):
        sent = jnp.where(to == (part * H + copy_at) // 3, piece[None], sent)
    last = swap(jnp.concatenate([out_term, sent], axis=1), COPY)
    grad_out = stacked(jnp.sum(last[:, : HS // 2].astype(F32), axis=0))
    blocks = [
        stacked(lax.dynamic_index_in_dim(last, (3 * copy_at + i) % COPIES, 0, False)[HS // 2 :])
        for i in range(3)
    ]
    grad_qkv = jnp.concatenate(blocks, axis=1).astype(F32)
    return (encoded[None, None], grad_qkv, grad_out)


def solution(mesh):
    fine = Mesh(mesh.devices.reshape(4, 2, 2, 8, 2), ("x", "y_lo", "core", "z", "y_hi"))
    in_specs = (
        P(CLIP, COPY, None),
        P(CLIP, COPY, None),
        P(CLIP, COPY, None),
        P(CLIP, COPY),
        P(CLIP, COPY, None),
        P(),
        P(CLIP, None),
        P(CLIP, None),
        P(),
        P(),
    )
    out_specs = (P(CLIP, COPY, None, None), P(CLIP, COPY), P(CLIP, COPY))
    return jax.shard_map(
        per_device, mesh=fine, in_specs=in_specs, out_specs=out_specs, check_vma=False
    )
```

```python
import jax
import jax.numpy as jnp
from jax import lax
from jax.experimental import pallas as pl
from jax.experimental.pallas import tpu as pltpu
from jax.sharding import Mesh
from jax.sharding import PartitionSpec as P


D = 1024
H = 16
HS = 64
HALF = HS // 2
L = 256
KMAX = 128
KW = 7
CLIPS = 16
COPIES = 16
ROWS = L // COPIES
QALL = COPIES * KMAX
NORM_EPSILON = 1e-05
MASKED_SCORE = -1e30
SCORE_SCALE = HS**-0.5
LOSS_SCALE = (KMAX * CLIPS * COPIES) ** -0.5
PAD = 8
LANES = 256
BLOCK = 128
VMEM_LIMIT = 20 * 1024 * 1024

XS, YS = 4, 2
CLIP = ("x", "y_lo", "core")
COPY = ("z", "y_hi")
F32 = jnp.float32
BF16 = jnp.bfloat16

VMEM = pl.BlockSpec(memory_space=pltpu.VMEM)
SMEM = pl.BlockSpec(memory_space=pltpu.SMEM)
HBM = pl.BlockSpec(memory_space=pltpu.HBM)


def mm(left, right):
    return jnp.dot(left, right, preferred_element_type=F32)


def mm_nt(left, right):
    return lax.dot_general(left, right, (((1,), (1,)), ((), ())), preferred_element_type=F32)


def call(kernel, name, microseconds, out_shape, in_specs, out_specs, scratch=()):
    return pl.pallas_call(
        kernel,
        out_shape=[
            pltpu.HBM(shape, dtype) if spec is HBM else jax.ShapeDtypeStruct(shape, dtype)
            for (shape, dtype), spec in zip(out_shape, out_specs)
        ],
        in_specs=in_specs,
        out_specs=out_specs,
        scratch_shapes=list(scratch),
        compiler_params=pltpu.CompilerParams(vmem_limit_bytes=VMEM_LIMIT),
        cost_estimate=pl.CostEstimate(
            flops=int(microseconds * 1e9), bytes_accessed=1024, transcendentals=0
        ),
        name=name,
    )


def pack_kernel(place_ref, count_ref, frames_ref, index_ref, w_ref, sent_ref, index_out, weights_ref, w_buf, sems):
    head = place_ref[0]
    copies = []
    for part in range(3):
        begin = pl.multiple_of(part * D + (head // 2) * BLOCK, BLOCK)
        copies.append(
            pltpu.make_async_copy(w_ref.at[:, pl.ds(begin, BLOCK)], w_buf.at[part], sems.at[part])
        )
        copies[part].start()
    lanes = lax.broadcasted_iota(jnp.int32, (ROWS, KMAX), 1)
    index = jnp.broadcast_to(index_ref[0], (ROWS, KMAX))
    index = jnp.where(lanes < count_ref[0, 0], index, L).astype(F32).astype(BF16)
    index_out[...] = index
    for m in range(COPIES):
        sent_ref[m, :, :D] = frames_ref[0]
        sent_ref[m, :, D:] = index
    odd = head % 2 == 1
    for part in range(3):
        copies[part].wait()
    q, k, v = [
        jnp.where(odd, w_buf[part, :, HS:].astype(F32), w_buf[part, :, :HS].astype(F32)) for part in range(3)
    ]
    weights_ref[:HS, :] = jnp.concatenate([q, k], axis=1).astype(BF16)
    weights_ref[HS:, :] = jnp.concatenate([v[:HALF], v[HALF:]], axis=1).astype(BF16)


def pack(place, count, frames, index, w_qkv):
    return call(
        pack_kernel,
        "pack",
        1,
        [((COPIES, ROWS, D + KMAX), BF16), ((ROWS, KMAX), BF16), ((HS + HALF, BLOCK), BF16)],
        [SMEM, SMEM, VMEM, VMEM, HBM],
        [VMEM, VMEM, VMEM],
        [pltpu.VMEM((3, HS, BLOCK), BF16), pltpu.SemaphoreType.DMA((3,))],
    )(place, count, frames, index, pltpu.with_memory_space_constraint(w_qkv, pltpu.HBM))


def normalize(got_ref, gain_ref):
    values = got_ref[:, :D].astype(F32)
    center = values - jnp.mean(values, axis=1, keepdims=True)
    spread = jnp.mean(center * center, axis=1, keepdims=True)
    return (center * lax.rsqrt(spread + NORM_EPSILON) * gain_ref[...]).astype(BF16)


def forward_kernel(
    got_ref, w_ref, gain_ref, targets_ref, out_ref, probs_out, pick_out, query_out, key_out, value_out,
    probs_ref, pick_ref, query_ref, wv_ref, sems,
):
    for m in range(COPIES):
        for a in range(D // BLOCK):
            rows = slice(HS + a * ROWS, HS + (a + 1) * ROWS)
            out_ref[m, rows, :] = targets_ref[0, :, a * BLOCK : (a + 1) * BLOCK]
    normed = normalize(got_ref, gain_ref)
    for c in range(CLIPS):
        wv_ref[c * HS : c * HS + HALF, :] = w_ref[c, HS:, :HS]
        wv_ref[c * HS + HALF : (c + 1) * HS, :] = w_ref[c, HS:, HS:]
    qk = mm(normed, w_ref[:, :HS, :].reshape(D, 2 * HS)).astype(BF16)
    v = mm(normed, wv_ref[...]).astype(BF16)
    qk_t = qk.astype(F32).T
    query_t = (qk_t[:HS] * SCORE_SCALE).astype(BF16)
    key = qk[:, HS:]
    key_out[...] = qk_t[HS:].astype(BF16)
    value_out[...] = v
    value_t = v.astype(F32).T.astype(BF16)
    rows = lax.broadcasted_iota(jnp.int32, (L, KMAX), 0).astype(F32)
    ones = jnp.ones((KMAX, KMAX), BF16)
    saves = []
    for m in range(COPIES):
        lanes = slice(m * KMAX, (m + 1) * KMAX)
        index = got_ref[m * ROWS : (m + 1) * ROWS, D:].astype(F32)[:1]
        pick = jnp.where(rows == index, 1.0, 0.0).astype(BF16)
        pick_ref[:, lanes] = pick
        queries = mm(query_t, pick).astype(BF16)
        query_ref[:, lanes] = queries
        scores = jnp.where(mm(pick, ones) > 0.5, mm(key, queries), MASKED_SCORE)
        raised = jnp.exp(scores - jnp.max(scores, axis=0, keepdims=True))
        probs = raised * (1.0 / jnp.sum(raised, axis=0, keepdims=True))
        probs_ref[m] = probs
        save = pltpu.make_async_copy(probs_ref.at[m], probs_out.at[m], sems.at[m])
        save.start()
        saves.append(save)
        out_ref[m, :HS, :] = mm(value_t, probs.astype(BF16)).astype(BF16)
    for here, there, at in ((pick_ref, pick_out, COPIES), (query_ref, query_out, COPIES + 1)):
        save = pltpu.make_async_copy(here, there, sems.at[at])
        save.start()
        saves.append(save)
    for save in saves:
        save.wait()


def forward(got, weights, gain, targets):
    return call(
        forward_kernel,
        "forward",
        6,
        [
            ((COPIES, HS + KMAX, KMAX), BF16),
            ((COPIES, L, KMAX), F32),
            ((L, QALL), BF16),
            ((HS, QALL), BF16),
            ((HS, L), BF16),
            ((L, HS), BF16),
        ],
        [VMEM] * 4,
        [VMEM, HBM, HBM, HBM, VMEM, VMEM],
        [
            pltpu.VMEM((COPIES, L, KMAX), F32),
            pltpu.VMEM((L, QALL), BF16),
            pltpu.VMEM((HS, QALL), BF16),
            pltpu.VMEM((D, HS), BF16),
            pltpu.SemaphoreType.DMA((COPIES + 2,)),
        ],
    )(got, weights, gain, targets)


def prepare_kernel(got_ref, gain_ref, out_ref, buf, sem):
    buf[...] = normalize(got_ref, gain_ref).T
    save = pltpu.make_async_copy(buf, out_ref, sem)
    save.start()
    save.wait()


def prepare(got, gain):
    return call(
        prepare_kernel,
        "prepare",
        2,
        [((D, L), BF16)],
        [VMEM] * 2,
        [HBM],
        [pltpu.VMEM((D, L), BF16), pltpu.SemaphoreType.DMA(())],
    )(got, gain)[0]


def decoder_kernel(
    place_ref, count_ref, recv_ref, got_ref, w_hbm, index_ref, embed_ref, taps_ref,
    encoded_ref, dctx_ref, ctx_ref, denc_ref, share_ref,
    w_ref, field_ref, sems,
):
    chunks = D // LANES
    copies = []
    for c in range(chunks):
        lanes = pl.ds(c * LANES, LANES)
        copies.append(pltpu.make_async_copy(w_hbm.at[:, lanes], w_ref.at[:, lanes], sems.at[c]))
        copies[c].start()
    core = place_ref[1]
    live = lax.broadcasted_iota(jnp.int32, (KMAX, 1), 0) < count_ref[0, 0]
    rows = lax.broadcasted_iota(jnp.int32, (L, KMAX), 0).astype(F32)
    hit = jnp.where(rows == index_ref[...].astype(F32)[:1], 1.0, 0.0)
    masked = 1.0 - jnp.sum(hit, axis=1, keepdims=True)
    place = hit.astype(BF16)
    pick = hit.T.astype(BF16)
    ctx_t = recv_ref[:, :HS, :]
    ctx_ref[...] = ctx_t
    ctx = ctx_t.reshape(D, KMAX).T
    for i in range(CLIPS // 2):
        share_ref[i, :HS, :] = ctx_ref[2 * i + 1 - core]
    reach = KW // 2
    field_ref[:PAD] = jnp.zeros((PAD, LANES), F32)
    field_ref[PAD + L :] = jnp.zeros((PAD, LANES), F32)
    for c in range(chunks):
        lanes = slice(c * LANES, (c + 1) * LANES)
        copies[c].wait()
        mixed = mm(pick, got_ref[:, lanes]) + mm(ctx, w_ref[:, lanes])
        encoded = jnp.where(live, mixed, 0.0).astype(BF16)
        encoded_ref[:, lanes] = encoded
        field_ref[PAD : PAD + L] = mm(place, encoded) + masked * embed_ref[:, lanes].astype(F32)
        predicted = taps_ref[:1, lanes] * field_ref[PAD - reach : PAD - reach + L]
        for t in range(1, KW):
            begin = PAD - reach + t
            predicted = predicted + taps_ref[t : t + 1, lanes] * field_ref[begin : begin + L]
        wanted = []
        for a in range(c * LANES // BLOCK, (c + 1) * LANES // BLOCK):
            block = recv_ref[:, HS + a * ROWS : HS + (a + 1) * ROWS, :]
            wanted.append(block.reshape(L, BLOCK))
        wanted = jnp.concatenate(wanted, axis=1).astype(F32)
        field_ref[PAD : PAD + L] = masked * (predicted - wanted) * LOSS_SCALE
        dfilled = taps_ref[:1, lanes] * field_ref[PAD + reach : PAD + reach + L]
        for t in range(1, KW):
            begin = PAD + reach - t
            dfilled = dfilled + taps_ref[t : t + 1, lanes] * field_ref[begin : begin + L]
        denc = mm(pick, dfilled.astype(BF16)).astype(BF16)
        denc_ref[:, lanes] = denc
        for a in range(c * LANES // BLOCK, (c + 1) * LANES // BLOCK):
            begin = a * BLOCK - c * LANES
            share_ref[a, HS:, :] = denc[:, begin : begin + BLOCK]
    dctx_ref[...] = mm_nt(w_ref[...], denc_ref[...]).astype(BF16)


def decoder(place, count, recv, got, w_out, index, embed, taps):
    return call(
        decoder_kernel,
        "decoder",
        5,
        [
            ((KMAX, D), BF16),
            ((D, KMAX), BF16),
            ((H, HS, KMAX), BF16),
            ((KMAX, D), BF16),
            ((CLIPS // 2, HS + KMAX, KMAX), BF16),
        ],
        [SMEM, SMEM, VMEM, VMEM, HBM, VMEM, VMEM, VMEM],
        [VMEM] * 5,
        [
            pltpu.VMEM((D, D), BF16),
            pltpu.VMEM((L + 2 * PAD, LANES), F32),
            pltpu.SemaphoreType.DMA((D // LANES,)),
        ],
    )(place, count, recv, got, pltpu.with_memory_space_constraint(w_out, pltpu.HBM), index, embed, taps)


def out_grad_kernel(place_ref, ctx_ref, denc_ref, share_ref, *refs):
    outs, both_ref = refs[:XS], refs[XS]
    core, x, y = place_ref[1], place_ref[2], place_ref[3]
    for a in range(D // BLOCK):
        lanes = slice(a * BLOCK, (a + 1) * BLOCK)
        both_ref[:KMAX, lanes] = denc_ref[:, lanes]
        both_ref[KMAX:, lanes] = share_ref[a, HS:, :]
    for r in range(XS):
        for s in range(YS):
            chip = YS * lax.rem(x + r, XS) + lax.rem(y + s, YS)
            left = jnp.concatenate([ctx_ref[2 * chip + core], share_ref[chip, :HS, :]], axis=1)
            block = mm(left, both_ref[...])
            upper, lower = block[:HALF], block[HALF:]
            for a in range(D // BLOCK):
                lanes = slice(a * BLOCK, (a + 1) * BLOCK)
                first, second = upper[:, lanes], lower[:, lanes]
                even = jnp.concatenate([first[:, :HS], second[:, :HS]], axis=1)
                odd = jnp.concatenate([first[:, HS:], second[:, HS:]], axis=1)
                outs[r][s, 2 * a] = even.astype(BF16)
                outs[r][s, 2 * a + 1] = odd.astype(BF16)


def out_grad(place, ctx, denc, share):
    return call(
        out_grad_kernel,
        "out_grad",
        1,
        [((YS, COPIES, HALF, BLOCK), BF16)] * XS,
        [SMEM] + [VMEM] * 3,
        [VMEM] * XS,
        [pltpu.VMEM((2 * KMAX, D), BF16)],
    )(place, ctx, denc, share)


def backward_kernel(
    dctx_ref, probs_ref, pick_ref, query_ref, key_ref, value_ref, normed_ref, out_ref, dctx_all, low_all, ds_all, dq_all
):
    key_t = key_ref[...]
    value = value_ref[...]
    for m in range(COPIES):
        lanes = slice(m * KMAX, (m + 1) * KMAX)
        dctx = dctx_ref[m]
        dctx_all[:, lanes] = dctx
        probs = probs_ref[m]
        low_all[:, lanes] = probs.astype(BF16)
        dprobs = mm(value, dctx)
        dscores = probs * (dprobs - jnp.sum(probs * dprobs, axis=0, keepdims=True))
        dscores = dscores.astype(BF16)
        ds_all[:, lanes] = dscores
        dq_all[:, lanes] = (mm(key_t, dscores) * SCORE_SCALE).astype(BF16)
    dvalue = mm_nt(dctx_all[...], low_all[...]).astype(BF16)
    dkey = mm_nt(query_ref[...], ds_all[...]).astype(BF16)
    dquery = mm_nt(dq_all[...], pick_ref[...]).astype(BF16)
    normed_t = normed_ref[...]
    grad_qk = mm_nt(normed_t, jnp.concatenate([dquery, dkey], axis=0)).astype(BF16)
    grad_v = mm_nt(normed_t, dvalue).astype(BF16)
    for c in range(CLIPS):
        out_ref[c, :HS, :] = grad_qk[c * HS : (c + 1) * HS]
        out_ref[c, HS:, :HS] = grad_v[c * HS : c * HS + HALF]
        out_ref[c, HS:, HS:] = grad_v[c * HS + HALF : (c + 1) * HS]


def backward(dctx, probs, pick, query, key, value, normed):
    return call(
        backward_kernel,
        "backward",
        5,
        [((CLIPS, HS + HALF, BLOCK), BF16)],
        [VMEM] * 7,
        [VMEM],
        [
            pltpu.VMEM((HS, QALL), BF16),
            pltpu.VMEM((L, QALL), BF16),
            pltpu.VMEM((L, QALL), BF16),
            pltpu.VMEM((HS, QALL), BF16),
        ],
    )(dctx, probs, pick, query, key, value, normed)[0]


def collect_kernel(place_ref, terms_ref, mine_ref, other_ref, out_ref):
    head = place_ref[0]
    out_ref[:, :HALF, :] = (mine_ref[...].astype(F32) + other_ref[...].astype(F32)).astype(BF16)
    out_ref[:, HALF:, :] = jnp.zeros((COPIES, HALF, BLOCK), BF16)
    term = jnp.sum(terms_ref[...].astype(F32), axis=0)
    upper, lower = term[:HALF], term[HALF:HS]
    query = jnp.concatenate([upper[:, :HS], lower[:, :HS]], axis=1)
    key = jnp.concatenate([upper[:, HS:], lower[:, HS:]], axis=1)
    for part, piece in enumerate((query, key, term[HS:])):
        out_ref[(part * H + head) // 3, HALF:, :] = piece.astype(BF16)


def collect(place, terms, mine, other):
    return call(
        collect_kernel,
        "collect",
        1,
        [((COPIES, HS, BLOCK), BF16)],
        [SMEM] + [VMEM] * 3,
        [VMEM],
    )(place, terms, mine, other)[0]


def finish_kernel(place_ref, last_ref, qkv_ref, out_ref):
    total = jnp.sum(last_ref[:, :HALF, :].astype(F32), axis=0)
    out_ref[:HALF, :] = total[:, :HS]
    out_ref[HALF:, :] = total[:, HS:]
    for i in range(3):
        block = last_ref[lax.rem(3 * place_ref[0] + i, COPIES), HALF:, :].astype(F32)
        qkv_ref[:HALF, i * HS : (i + 1) * HS] = block[:, :HS]
        qkv_ref[HALF:, i * HS : (i + 1) * HS] = block[:, HS:]


def finish(place, last):
    return call(
        finish_kernel,
        "finish",
        1,
        [((HS, 3 * HS), F32), ((HS, HS), F32)],
        [SMEM, VMEM],
        [VMEM] * 2,
    )(place, last)


def swap(array, axes):
    return lax.all_to_all(array, axes, 0, 0, tiled=True)


def total(*parts):
    result = parts[0].astype(F32)
    for part in parts[1:]:
        result = result + part.astype(F32)
    return result.astype(BF16)


def per_device(
    frames,
    targets,
    kept_index,
    kept_count,
    fill_slot,
    norm_gain,
    w_qkv,
    w_out,
    mask_embed,
    dec_kernel,
):
    place = jnp.stack(
        [lax.axis_index(COPY), lax.axis_index("core"), lax.axis_index("x"), lax.axis_index("y_lo")]
    )
    gain = norm_gain[None, :]
    sent, index, weights = pack(place, kept_count, frames, kept_index, w_qkv)
    got = swap(sent, COPY).reshape(L, D + KMAX)
    for axis in ("core", "y_lo", "x"):
        weights = lax.all_gather(weights, axis, axis=0)
    weights = weights.reshape(CLIPS, HS + HALF, BLOCK)
    w_out_all = lax.all_gather(w_out, CLIP, axis=0, tiled=True)

    sent, probs, pick, query, key, value = forward(got, weights, gain, targets)
    normed = prepare(got, gain)
    recv = swap(sent, COPY)
    encoded, dctx, ctx, denc, share = decoder(
        place, kept_count, recv, got, w_out_all, index, mask_embed[None, :], dec_kernel
    )
    dctx = swap(dctx.reshape(H, HS, KMAX), COPY)

    share = lax.ppermute(share, "core", [(0, 1), (1, 0)])
    parts = list(out_grad(place, ctx, denc, share))
    for r in range(1, XS):
        parts[r] = lax.ppermute(parts[r], "x", [(i, (i + r) % XS) for i in range(XS)])
    mine = total(*[part[0] for part in parts])
    other = total(*[part[1] for part in parts])
    other = lax.ppermute(other, "y_lo", [(0, 1), (1, 0)])

    terms = swap(backward(dctx, probs, pick, query, key, value, normed), CLIP)
    grad_qkv, grad_out = finish(place, swap(collect(place, terms, mine, other), COPY))
    return (encoded[None, None], grad_qkv, grad_out)


def solution(mesh):
    fine = Mesh(mesh.devices.reshape(XS, YS, 2, 8, 2), ("x", "y_lo", "core", "z", "y_hi"))
    in_specs = (
        P(CLIP, COPY, None),
        P(CLIP, COPY, None),
        P(CLIP, COPY, None),
        P(CLIP, COPY),
        P(CLIP, COPY, None),
        P(),
        P(CLIP, None),
        P(CLIP, None),
        P(),
        P(),
    )
    out_specs = (P(CLIP, COPY, None, None), P(CLIP, COPY), P(CLIP, COPY))
    return jax.shard_map(
        per_device, mesh=fine, in_specs=in_specs, out_specs=out_specs, check_vma=False
    )
```

```python
import jax
import jax.numpy as jnp
from jax import lax
from jax.experimental import pallas as pl
from jax.experimental.pallas import tpu as pltpu
from jax.sharding import Mesh
from jax.sharding import PartitionSpec as P


D = 1024
H = 16
HS = 64
HALF = HS // 2
L = 256
KMAX = 128
KW = 7
CLIPS = 16
COPIES = 16
QALL = COPIES * KMAX
NORM_EPSILON = 1e-05
MASKED_SCORE = -1e30
SCORE_SCALE = HS**-0.5
ROWS = L // COPIES
LOSS_SCALE = (KMAX * CLIPS * COPIES) ** -0.5
PAD = 8
LANES = 256
BLOCK = 128
EARLY = D // 2
LATE = (D - EARLY) // BLOCK * ROWS
QKV = HS + HALF
EXTRA = 16
GROUP = 8
VMEM_LIMIT = 20 * 1024 * 1024

XS, YS = 4, 2
CLIP = ("x", "y_lo", "core")
COPY = ("z", "y_hi")
F32 = jnp.float32
BF16 = jnp.bfloat16

VMEM = pl.BlockSpec(memory_space=pltpu.VMEM)
SMEM = pl.BlockSpec(memory_space=pltpu.SMEM)
HBM = pl.BlockSpec(memory_space=pltpu.HBM)


def mm(left, right):
    return jnp.dot(left, right, preferred_element_type=F32)


def mm_nt(left, right):
    return lax.dot_general(left, right, (((1,), (1,)), ((), ())), preferred_element_type=F32)


def call(kernel, name, microseconds, out_shape, in_specs, out_specs, scratch=()):
    return pl.pallas_call(
        kernel,
        out_shape=[
            pltpu.HBM(shape, dtype) if spec is HBM else jax.ShapeDtypeStruct(shape, dtype)
            for (shape, dtype), spec in zip(out_shape, out_specs)
        ],
        in_specs=in_specs,
        out_specs=out_specs,
        scratch_shapes=list(scratch),
        compiler_params=pltpu.CompilerParams(vmem_limit_bytes=VMEM_LIMIT),
        cost_estimate=pl.CostEstimate(
            flops=int(microseconds * 1e9), bytes_accessed=1024, transcendentals=0
        ),
        name=name,
    )


def in_hbm(array):
    return pltpu.with_memory_space_constraint(array, pltpu.HBM)


def pack_kernel(
    place_ref, count_ref, frames_hbm, targets_hbm, index_hbm, w_ref, wo_hbm,
    sent_ref, index_out, weights_ref, w_buf, wo_buf, frames_ref, targets_ref, index_ref, sems,
):
    head = place_ref[0]
    copies = []
    load_index = pltpu.make_async_copy(index_hbm.at[0], index_ref, sems.at[3])
    load_index.start()
    load_frames = pltpu.make_async_copy(frames_hbm.at[0], frames_ref, sems.at[4])
    load_frames.start()
    load_targets = pltpu.make_async_copy(targets_hbm.at[0, :, :EARLY], targets_ref, sems.at[6])
    load_targets.start()
    load_out = pltpu.make_async_copy(wo_hbm, wo_buf, sems.at[5])
    load_out.start()
    for part in range(3):
        begin = pl.multiple_of(part * D + (head // 2) * BLOCK, BLOCK)
        copies.append(
            pltpu.make_async_copy(w_ref.at[:, pl.ds(begin, BLOCK)], w_buf.at[part], sems.at[part])
        )
        copies[part].start()
    lanes = lax.broadcasted_iota(jnp.int32, (ROWS, KMAX), 1)
    load_index.wait()
    index = jnp.broadcast_to(index_ref[...], (ROWS, KMAX))
    index = jnp.where(lanes < count_ref[0, 0], index, L).astype(F32).astype(BF16)
    index_out[...] = index
    load_frames.wait()
    load_targets.wait()
    for m in range(COPIES):
        sent_ref[m, :, :D] = frames_ref[...]
        sent_ref[m, :, D : D + KMAX] = index
        sent_ref[m, :, D + KMAX :] = targets_ref[...]
    odd = head % 2 == 1
    for part in range(3):
        copies[part].wait()
    q, k, v = [
        jnp.where(odd, w_buf[part, :, HS:].astype(F32), w_buf[part, :, :HS].astype(F32)) for part in range(3)
    ]
    weights_ref[:HS, :] = jnp.concatenate([q, k], axis=1).astype(BF16)
    weights_ref[HS:QKV, :] = jnp.concatenate([v[:HALF], v[HALF:]], axis=1).astype(BF16)
    load_out.wait()
    for a in range(D // BLOCK):
        weights_ref[QKV + a * HS : QKV + (a + 1) * HS, :] = wo_buf[:, a * BLOCK : (a + 1) * BLOCK]


def pack(place, count, frames, targets, index, w_qkv, w_out):
    return call(
        pack_kernel,
        "pack",
        1,
        [((COPIES, ROWS, D + KMAX + EARLY), BF16), ((ROWS, KMAX), BF16), ((QKV + HS * D // BLOCK, BLOCK), BF16)],
        [SMEM, SMEM] + [HBM] * 5,
        [VMEM, VMEM, VMEM],
        [
            pltpu.VMEM((3, HS, BLOCK), BF16),
            pltpu.VMEM((HS, D), BF16),
            pltpu.VMEM((ROWS, D), BF16),
            pltpu.VMEM((ROWS, EARLY), BF16),
            pltpu.VMEM((1, KMAX), jnp.int32),
            pltpu.SemaphoreType.DMA((7,)),
        ],
    )(place, count, in_hbm(frames), in_hbm(targets), in_hbm(index), in_hbm(w_qkv), in_hbm(w_out))


def normalize(got_ref, gain_hbm, gain_ref, sem):
    load = pltpu.make_async_copy(gain_hbm, gain_ref, sem)
    load.start()
    values = got_ref[:, :D].astype(F32)
    center = values - jnp.mean(values, axis=1, keepdims=True)
    spread = jnp.mean(center * center, axis=1, keepdims=True)
    load.wait()
    return (center * lax.rsqrt(spread + NORM_EPSILON) * gain_ref[...]).astype(BF16)


def forward_kernel(
    got_ref, w_ref, gain_hbm, targets_ref, out_ref, probs_out, pick_out, qkv_out,
    probs_ref, pick_ref, qkv_ref, wqk_ref, wv_ref, gain_ref, sems,
):
    for m in range(COPIES):
        for a in range((D - EARLY) // BLOCK):
            lanes = slice(EARLY + a * BLOCK, EARLY + (a + 1) * BLOCK)
            out_ref[m, HS + a * ROWS : HS + (a + 1) * ROWS, :] = targets_ref[0, :, lanes]
    normed = normalize(got_ref, gain_hbm, gain_ref, sems.at[3 * COPIES // GROUP])
    for c in range(CLIPS):
        block = w_ref[c % 2, c // (2 * YS), c // 2 % YS]
        wqk_ref[c * HS : (c + 1) * HS, :] = block[:HS]
        wv_ref[c * HS : c * HS + HALF, :] = block[HS:, :HS]
        wv_ref[c * HS + HALF : (c + 1) * HS, :] = block[HS:, HS:]
    qk = mm(normed, wqk_ref[...]).astype(BF16).astype(F32)
    v = mm(normed, wv_ref[...]).astype(BF16).astype(F32)
    qk_t = qk.T
    qkv_t = jnp.concatenate([qk_t[:HS] * SCORE_SCALE, qk_t[HS:], v.T], axis=0).astype(BF16)
    rows = lax.broadcasted_iota(jnp.int32, (L, KMAX), 0).astype(F32)
    first = lax.broadcasted_iota(jnp.int32, (EXTRA, KMAX), 0) == 0
    one_row = jnp.where(first, 1.0, 0.0).astype(BF16)
    saves = []
    for begin in range(0, COPIES, GROUP):
        group = range(begin, begin + GROUP)
        index = [got_ref[m * ROWS : (m + 1) * ROWS, D : D + KMAX].astype(F32)[:1] for m in group]
        pick = [jnp.where(rows == i, 1.0, 0.0).astype(BF16) for i in index]
        for m, p in zip(group, pick):
            pick_ref[:, m * KMAX : (m + 1) * KMAX] = p
        qkv = [mm(qkv_t, p).astype(BF16) for p in pick]
        for m, a in zip(group, qkv):
            qkv_ref[m] = a
        bias = [jnp.where(first & (i > L - 0.5), MASKED_SCORE, 0.0).astype(BF16) for i in index]
        queries = [jnp.concatenate([a[:HS], one_row], axis=0) for a in qkv]
        keys = [jnp.concatenate([a[HS : 2 * HS], e], axis=0).T for a, e in zip(qkv, bias)]
        scores = [mm(k, q) for k, q in zip(keys, queries)]
        raised = [jnp.exp(a - jnp.max(a, axis=0, keepdims=True)) for a in scores]
        probs = [a * (1.0 / jnp.sum(a, axis=0, keepdims=True)) for a in raised]
        for m, p in zip(group, probs):
            probs_ref[m] = p
        ctx = [mm(a[2 * HS :], p.astype(BF16)) for a, p in zip(qkv, probs)]
        for m, a in zip(group, ctx):
            out_ref[m, :HS, :] = a.astype(BF16)
        part = pl.ds(begin, GROUP)
        lanes = pl.ds(begin * KMAX, GROUP * KMAX)
        for here, there in (
            (probs_ref.at[part], probs_out.at[part]),
            (qkv_ref.at[part], qkv_out.at[part]),
            (pick_ref.at[:, lanes], pick_out.at[:, lanes]),
        ):
            saves.append(pltpu.make_async_copy(here, there, sems.at[len(saves)]))
            saves[-1].start()
    for save in saves:
        save.wait()


def forward(got, weights, gain, targets):
    return call(
        forward_kernel,
        "forward",
        0.1,
        [
            ((COPIES, HS + LATE, KMAX), BF16),
            ((COPIES, KMAX, KMAX), F32),
            ((L, QALL), BF16),
            ((COPIES, 3 * HS, KMAX), BF16),
        ],
        [VMEM, VMEM, HBM, VMEM],
        [VMEM, HBM, HBM, HBM],
        [
            pltpu.VMEM((COPIES, KMAX, KMAX), F32),
            pltpu.VMEM((L, QALL), BF16),
            pltpu.VMEM((COPIES, 3 * HS, KMAX), BF16),
            pltpu.VMEM((D, 2 * HS), BF16),
            pltpu.VMEM((D, HS), BF16),
            pltpu.VMEM((1, D), F32),
            pltpu.SemaphoreType.DMA((3 * COPIES // GROUP + 1,)),
        ],
    )(got, weights, in_hbm(gain), targets)


def prepare_kernel(got_ref, gain_hbm, out_ref, buf, gain_ref, sems):
    buf[...] = normalize(got_ref, gain_hbm, gain_ref, sems.at[1]).T
    save = pltpu.make_async_copy(buf, out_ref, sems.at[0])
    save.start()
    save.wait()


def prepare(got, gain):
    return call(
        prepare_kernel,
        "prepare",
        2,
        [((D, L), BF16)],
        [VMEM, HBM],
        [HBM],
        [pltpu.VMEM((D, L), BF16), pltpu.VMEM((1, D), F32), pltpu.SemaphoreType.DMA((2,))],
    )(got, in_hbm(gain))[0]


def decoder_kernel(
    place_ref, count_ref, recv_ref, got_ref, index_ref, embed_ref, taps_ref, *refs
):
    w_refs = refs[: 2 * XS]
    encoded_ref, dctx_ref, ctx_out, denc_out, share_out = refs[2 * XS : 2 * XS + 5]
    ctx_ref, denc_ref, share_ref, field_ref, error_ref, dfilled_ref, sems = refs[2 * XS + 5 :]
    chunks = D // LANES
    core, x = place_ref[1], place_ref[2]
    parts = []
    for s in range(XS):
        chip = YS * lax.rem(x + XS - s, XS)
        clips = [2 * (chip + t) + side for side in (core, 1 - core) for t in range(YS)]
        weights = [
            jnp.concatenate(
                [w_refs[s][:, a].reshape(YS * HS, BLOCK), w_refs[XS + s][:, a].reshape(YS * HS, BLOCK)], axis=0
            )
            for a in range(D // BLOCK)
        ]
        parts.append((clips, weights))
    live = lax.broadcasted_iota(jnp.int32, (KMAX, 1), 0) < count_ref[0, 0]
    rows = lax.broadcasted_iota(jnp.int32, (L, KMAX), 0).astype(F32)
    hit = jnp.where(rows == index_ref[...].astype(F32)[:1], 1.0, 0.0)
    masked = 1.0 - jnp.sum(hit, axis=1, keepdims=True)
    place = hit.astype(BF16)
    pick = hit.T.astype(BF16)
    ctx_ref[...] = recv_ref[:, :HS, :]
    saves = [
        pltpu.make_async_copy(here, there, sems.at[at])
        for at, (here, there) in enumerate(
            ((ctx_ref, ctx_out), (denc_ref, denc_out), (share_ref, share_out))
        )
    ]
    saves[0].start()
    ctx = [
        jnp.concatenate([ctx_ref[clip] for clip in clips], axis=0).T for clips, weights in parts
    ]
    for i in range(CLIPS // 2):
        share_ref[i, :HS, :] = ctx_ref[2 * i + 1 - core]
    reach = KW // 2
    blocks = D // BLOCK
    for ref in (field_ref, error_ref):
        ref[:PAD] = jnp.zeros((PAD, D), F32)
        ref[PAD + L :] = jnp.zeros((PAD, D), F32)
    inside = slice(PAD, PAD + L)
    columns = [slice(c * LANES, (c + 1) * LANES) for c in range(chunks)]
    inputs = [mm(pick, got_ref[:, lanes]) for lanes in columns]
    per = LANES // BLOCK
    mixed = inputs
    for left, (clips, weights) in zip(ctx, parts):
        wide = [
            jnp.concatenate(weights[c * per : (c + 1) * per], axis=1) for c in range(chunks)
        ]
        mixed = [m + mm(left, w) for m, w in zip(mixed, wide)]
    encoded = [jnp.where(live, m, 0.0).astype(BF16) for m in mixed]
    for lanes, e in zip(columns, encoded):
        encoded_ref[:, lanes] = e
    for lanes, e in zip(columns, encoded):
        field_ref[inside, lanes] = mm(place, e) + masked * embed_ref[:, lanes].astype(F32)
    for a in range(blocks):
        lanes = slice(a * BLOCK, (a + 1) * BLOCK)
        predicted = taps_ref[:1, lanes] * field_ref[PAD - reach : PAD - reach + L, lanes]
        for t in range(1, KW):
            begin = PAD - reach + t
            predicted = predicted + taps_ref[t : t + 1, lanes] * field_ref[begin : begin + L, lanes]
        if (a + 1) * BLOCK <= EARLY:
            begin = D + KMAX + a * BLOCK
            wanted = got_ref[:, begin : begin + BLOCK]
        else:
            begin = HS + (a * BLOCK - EARLY) // BLOCK * ROWS
            wanted = recv_ref[:, begin : begin + ROWS, :].reshape(L, BLOCK)
        error_ref[inside, lanes] = masked * (predicted - wanted.astype(F32)) * LOSS_SCALE
    for a in range(blocks):
        lanes = slice(a * BLOCK, (a + 1) * BLOCK)
        dfilled = taps_ref[:1, lanes] * error_ref[PAD + reach : PAD + reach + L, lanes]
        for t in range(1, KW):
            begin = PAD + reach - t
            dfilled = dfilled + taps_ref[t : t + 1, lanes] * error_ref[begin : begin + L, lanes]
        dfilled_ref[:, lanes] = dfilled.astype(BF16)
    denc = [mm(pick, dfilled_ref[:, lanes]).astype(BF16) for lanes in columns]
    for c in range(chunks):
        denc_ref[:, columns[c]] = denc[c]
        for i in range(per):
            share_ref[c * per + i, HS:, :] = denc[c][:, i * BLOCK : (i + 1) * BLOCK]
    saves[1].start()
    saves[2].start()
    denc = denc_ref[...]
    for clips, weights in parts:
        dctx = mm_nt(jnp.concatenate(weights, axis=1), denc).astype(BF16)
        for r, clip in enumerate(clips):
            dctx_ref[clip] = dctx[r * HS : (r + 1) * HS]
    for save in saves:
        save.wait()


def decoder(place, count, recv, got, w_out, index, embed, taps):
    return call(
        decoder_kernel,
        "decoder",
        5,
        [
            ((KMAX, D), BF16),
            ((H, HS, KMAX), BF16),
            ((H, HS, KMAX), BF16),
            ((KMAX, D), BF16),
            ((CLIPS // 2, HS + KMAX, KMAX), BF16),
        ],
        [SMEM, SMEM] + [VMEM] * (5 + 2 * XS),
        [VMEM] * 2 + [HBM] * 3,
        [
            pltpu.VMEM((H, HS, KMAX), BF16),
            pltpu.VMEM((KMAX, D), BF16),
            pltpu.VMEM((CLIPS // 2, HS + KMAX, KMAX), BF16),
            pltpu.VMEM((L + 2 * PAD, D), F32),
            pltpu.VMEM((L + 2 * PAD, D), F32),
            pltpu.VMEM((L, D), BF16),
            pltpu.SemaphoreType.DMA((3,)),
        ],
    )(place, count, recv, got, index, embed, taps, *w_out)


def out_grad_kernel(place_ref, ctx_ref, denc_ref, share_ref, *refs):
    outs, both_ref = refs[:XS], refs[XS]
    core, x, y = place_ref[1], place_ref[2], place_ref[3]
    for a in range(D // BLOCK):
        lanes = slice(a * BLOCK, (a + 1) * BLOCK)
        both_ref[:KMAX, lanes] = denc_ref[:, lanes]
        both_ref[KMAX:, lanes] = share_ref[a, HS:, :]
    for r in range(XS):
        for s in range(YS):
            chip = YS * lax.rem(x + r, XS) + lax.rem(y + s, YS)
            left = jnp.concatenate([ctx_ref[2 * chip + core], share_ref[chip, :HS, :]], axis=1)
            block = mm(left, both_ref[...])
            upper, lower = block[:HALF], block[HALF:]
            for a in range(D // BLOCK):
                lanes = slice(a * BLOCK, (a + 1) * BLOCK)
                first, second = upper[:, lanes], lower[:, lanes]
                even = jnp.concatenate([first[:, :HS], second[:, :HS]], axis=1)
                odd = jnp.concatenate([first[:, HS:], second[:, HS:]], axis=1)
                outs[r][s, 2 * a] = even.astype(BF16)
                outs[r][s, 2 * a + 1] = odd.astype(BF16)


def out_grad(place, ctx, denc, share):
    return call(
        out_grad_kernel,
        "out_grad",
        1,
        [((YS, COPIES, HALF, BLOCK), BF16)] * XS,
        [SMEM] + [VMEM] * 3,
        [VMEM] * XS,
        [pltpu.VMEM((2 * KMAX, D), BF16)],
    )(place, ctx, denc, share)


def backward_kernel(
    dctx_ref, probs_hbm, pick_hbm, qkv_hbm, normed_hbm, out_ref,
    probs_ref, pick_ref, qkv_ref, normed_ref, dqkv_ref, sems,
):
    loads = []
    for at, (there, here) in enumerate(
        ((qkv_hbm, qkv_ref), (probs_hbm, probs_ref), (pick_hbm, pick_ref), (normed_hbm, normed_ref))
    ):
        loads.append(pltpu.make_async_copy(there, here, sems.at[at]))
        loads[at].start()
    loads[0].wait()
    loads[1].wait()
    for begin in range(0, COPIES, GROUP):
        group = range(begin, begin + GROUP)
        dctx = [dctx_ref[m] for m in group]
        qkv = [qkv_ref[m] for m in group]
        probs = [probs_ref[m] for m in group]
        dprobs = [mm(a[2 * HS :].T, d) for a, d in zip(qkv, dctx)]
        along = [jnp.sum(p * d, axis=0, keepdims=True) for p, d in zip(probs, dprobs)]
        dscores = [(p * (d - a)).astype(BF16) for p, d, a in zip(probs, dprobs, along)]
        dvalue = [mm(p.astype(BF16), d.T) for p, d in zip(probs, dctx)]
        dkey = [mm(d, a[:HS].T) for d, a in zip(dscores, qkv)]
        dquery = [(mm(a[HS : 2 * HS], d) * SCORE_SCALE).T for a, d in zip(qkv, dscores)]
        for m, q, k, v in zip(group, dquery, dkey, dvalue):
            dqkv = jnp.concatenate([q, k, v], axis=1)
            dqkv_ref[m * KMAX : (m + 1) * KMAX, :] = dqkv.astype(BF16)
    loads[2].wait()
    loads[3].wait()
    total = mm(pick_ref[...], dqkv_ref[...]).astype(BF16)
    grad = mm(normed_ref[...], total).astype(BF16)
    for c in range(CLIPS):
        block = grad[c * HS : (c + 1) * HS]
        out_ref[c, :HS, :] = block[:, : 2 * HS]
        out_ref[c, HS:, :HS] = block[:HALF, 2 * HS :]
        out_ref[c, HS:, HS:] = block[HALF:, 2 * HS :]


def backward(dctx, probs, pick, qkv, normed):
    return call(
        backward_kernel,
        "backward",
        5,
        [((CLIPS, HS + HALF, BLOCK), BF16)],
        [VMEM] + [HBM] * 4,
        [VMEM],
        [
            pltpu.VMEM((COPIES, KMAX, KMAX), F32),
            pltpu.VMEM((L, QALL), BF16),
            pltpu.VMEM((COPIES, 3 * HS, KMAX), BF16),
            pltpu.VMEM((D, L), BF16),
            pltpu.VMEM((QALL, 3 * HS), BF16),
            pltpu.SemaphoreType.DMA((4,)),
        ],
    )(dctx, in_hbm(probs), in_hbm(pick), in_hbm(qkv), in_hbm(normed))[0]


def collect_kernel(place_ref, terms_ref, mine_ref, other_ref, out_ref):
    head = place_ref[0]
    out_ref[:, :HALF, :] = (mine_ref[...].astype(F32) + other_ref[...].astype(F32)).astype(BF16)
    out_ref[:, HALF:, :] = jnp.zeros((COPIES, HALF, BLOCK), BF16)
    term = jnp.sum(terms_ref[...].astype(F32), axis=0)
    upper, lower = term[:HALF], term[HALF:HS]
    query = jnp.concatenate([upper[:, :HS], lower[:, :HS]], axis=1)
    key = jnp.concatenate([upper[:, HS:], lower[:, HS:]], axis=1)
    for part, piece in enumerate((query, key, term[HS:])):
        out_ref[(part * H + head) // 3, HALF:, :] = piece.astype(BF16)


def collect(place, terms, mine, other):
    return call(
        collect_kernel,
        "collect",
        1,
        [((COPIES, HS, BLOCK), BF16)],
        [SMEM] + [VMEM] * 3,
        [VMEM],
    )(place, terms, mine, other)[0]


def finish_kernel(place_ref, last_ref, qkv_ref, out_ref):
    total = jnp.sum(last_ref[:, :HALF, :].astype(F32), axis=0)
    out_ref[:HALF, :] = total[:, :HS]
    out_ref[HALF:, :] = total[:, HS:]
    for i in range(3):
        block = last_ref[lax.rem(3 * place_ref[0] + i, COPIES), HALF:, :].astype(F32)
        qkv_ref[:HALF, i * HS : (i + 1) * HS] = block[:, :HS]
        qkv_ref[HALF:, i * HS : (i + 1) * HS] = block[:, HS:]


def finish(place, last):
    return call(
        finish_kernel,
        "finish",
        1,
        [((HS, 3 * HS), F32), ((HS, HS), F32)],
        [SMEM, VMEM],
        [VMEM] * 2,
    )(place, last)


def swap(array, axes):
    return lax.all_to_all(array, axes, 0, 0, tiled=True)


def total(*parts):
    result = parts[0].astype(F32)
    for part in parts[1:]:
        result = result + part.astype(F32)
    return result.astype(BF16)


def per_device(
    frames,
    targets,
    kept_index,
    kept_count,
    fill_slot,
    norm_gain,
    w_qkv,
    w_out,
    mask_embed,
    dec_kernel,
):
    place = jnp.stack(
        [lax.axis_index(COPY), lax.axis_index("core"), lax.axis_index("x"), lax.axis_index("y_lo")]
    )
    gain = norm_gain[None, :]
    sent, index, weights = pack(place, kept_count, frames, targets, kept_index, w_qkv, w_out)
    got = swap(sent, COPY).reshape(L, D + KMAX + EARLY)
    weights = lax.all_gather(weights, "y_lo", axis=0)
    near = weights[:, QKV:].reshape(YS, D // BLOCK, HS, BLOCK)
    weights = weights[:, :QKV]
    for axis in ("x", "core"):
        weights = lax.all_gather(weights, axis, axis=0)

    sent, probs, pick, qkv = forward(got, weights, gain, targets)
    normed = prepare(got, gain)
    recv = swap(sent, COPY)
    near, sent = lax.optimization_barrier((near, sent))
    w_out = [near]
    for r in range(1, XS):
        w_out.append(lax.ppermute(near, "x", [(i, (i + r) % XS) for i in range(XS)]))
    w_out += [lax.ppermute(part, "core", [(0, 1), (1, 0)]) for part in w_out]
    encoded, dctx, ctx, denc, share = decoder(
        place, kept_count, recv, got, w_out, index, mask_embed[None, :], dec_kernel
    )
    dctx = swap(dctx, COPY)

    share = lax.ppermute(share, "core", [(0, 1), (1, 0)])
    parts = list(out_grad(place, ctx, denc, share))
    for r in range(1, XS):
        parts[r] = lax.ppermute(parts[r], "x", [(i, (i + r) % XS) for i in range(XS)])
    mine = total(*[part[0] for part in parts])
    other = total(*[part[1] for part in parts])
    other = lax.ppermute(other, "y_lo", [(0, 1), (1, 0)])

    terms = swap(backward(dctx, probs, pick, qkv, normed), CLIP)
    grad_qkv, grad_out = finish(place, swap(collect(place, terms, mine, other), COPY))
    return (encoded[None, None], grad_qkv, grad_out)


def solution(mesh):
    fine = Mesh(mesh.devices.reshape(XS, YS, 2, 8, 2), ("x", "y_lo", "core", "z", "y_hi"))
    in_specs = (
        P(CLIP, COPY, None),
        P(CLIP, COPY, None),
        P(CLIP, COPY, None),
        P(CLIP, COPY),
        P(CLIP, COPY, None),
        P(),
        P(CLIP, None),
        P(CLIP, None),
        P(),
        P(),
    )
    out_specs = (P(CLIP, COPY, None, None), P(CLIP, COPY), P(CLIP, COPY))
    return jax.shard_map(
        per_device, mesh=fine, in_specs=in_specs, out_specs=out_specs, check_vma=False
    )
```

```python
import jax
import jax.numpy as jnp
from jax import lax
from jax.experimental import pallas as pl
from jax.experimental.pallas import tpu as pltpu
from jax.sharding import Mesh
from jax.sharding import PartitionSpec as P


D = 1024
H = 16
HS = 64
HALF = HS // 2
L = 256
KMAX = 128
KW = 7
CLIPS = 16
COPIES = 16
QALL = COPIES * KMAX
NORM_EPSILON = 1e-05
MASKED_SCORE = -1e30
SCORE_SCALE = HS**-0.5
ROWS = L // COPIES
LOSS_SCALE = (KMAX * CLIPS * COPIES) ** -0.5
PAD = 8
LANES = 256
BLOCK = 128
EARLY = D // 4
LATE = (D - EARLY) // BLOCK * ROWS
QKV = HS + HALF
EXTRA = 16
GROUP = 8
VMEM_LIMIT = 20 * 1024 * 1024

XS, YS = 4, 2
CLIP = ("x", "y_lo", "core")
COPY = ("z", "y_hi")
RING = ("y_hi", "z")
ZS, ZY = 8, 2
F32 = jnp.float32
BF16 = jnp.bfloat16

VMEM = pl.BlockSpec(memory_space=pltpu.VMEM)
HBM = pl.BlockSpec(memory_space=pltpu.HBM)


def slot(copy):
    return copy % ZY * ZS + copy // ZY


def copy_of(place):
    return place % ZS * ZY + place // ZS


def in_order(blocks):
    return jnp.concatenate([blocks(slot(copy)) for copy in range(COPIES)], axis=0)


def frame_ids(width):
    row = lax.broadcasted_iota(jnp.int32, (L, width), 0)
    return (copy_of(row // ROWS) * ROWS + row % ROWS).astype(F32)


def head_here():
    return lax.axis_index("z") * ZY + lax.axis_index("y_hi")


def mm(left, right):
    return jnp.dot(left, right, preferred_element_type=F32)


def mm_nt(left, right):
    return lax.dot_general(left, right, (((1,), (1,)), ((), ())), preferred_element_type=F32)


def call(kernel, name, microseconds, out_shape, in_specs, out_specs, scratch=()):
    return pl.pallas_call(
        kernel,
        out_shape=[
            pltpu.HBM(shape, dtype) if spec is HBM else jax.ShapeDtypeStruct(shape, dtype)
            for (shape, dtype), spec in zip(out_shape, out_specs)
        ],
        in_specs=in_specs,
        out_specs=out_specs,
        scratch_shapes=list(scratch),
        compiler_params=pltpu.CompilerParams(vmem_limit_bytes=VMEM_LIMIT),
        cost_estimate=pl.CostEstimate(
            flops=int(microseconds * 1e9), bytes_accessed=1024, transcendentals=0
        ),
        name=name,
    )


def in_hbm(array):
    return pltpu.with_memory_space_constraint(array, pltpu.HBM)


def pack_kernel(
    slots_hbm, frames_hbm, targets_hbm, index_hbm, w_ref, wo_hbm,
    sent_ref, index_out, weights_ref, w_buf, wo_buf, frames_ref, targets_ref, index_ref, slots_ref, sems,
):
    head = head_here()
    copies = []
    load_index = pltpu.make_async_copy(index_hbm.at[0], index_ref, sems.at[3])
    load_index.start()
    load_slots = pltpu.make_async_copy(slots_hbm.at[0], slots_ref, sems.at[7])
    load_slots.start()
    load_frames = pltpu.make_async_copy(frames_hbm.at[0], frames_ref, sems.at[4])
    load_frames.start()
    load_targets = pltpu.make_async_copy(targets_hbm.at[0, :, :EARLY], targets_ref, sems.at[6])
    load_targets.start()
    load_out = pltpu.make_async_copy(wo_hbm, wo_buf, sems.at[5])
    load_out.start()
    for part in range(3):
        begin = pl.multiple_of(part * D + (head // 2) * BLOCK, BLOCK)
        copies.append(
            pltpu.make_async_copy(w_ref.at[:, pl.ds(begin, BLOCK)], w_buf.at[part], sems.at[part])
        )
        copies[part].start()
    lanes = lax.broadcasted_iota(jnp.int32, (ROWS, KMAX), 1)
    load_index.wait()
    load_slots.wait()
    kept = jnp.where(slots_ref[...] < KMAX, 1.0, 0.0)
    count = jnp.sum(kept, axis=1, keepdims=True)
    index = jnp.broadcast_to(index_ref[...], (ROWS, KMAX))
    index = jnp.where(lanes.astype(F32) < count, index, L).astype(F32).astype(BF16)
    index_out[...] = index
    load_frames.wait()
    load_targets.wait()
    for m in range(COPIES):
        sent_ref[m, :, :D] = frames_ref[...]
        sent_ref[m, :, D : D + KMAX] = index
        sent_ref[m, :, D + KMAX :] = targets_ref[...]
    odd = head % 2 == 1
    for part in range(3):
        copies[part].wait()
    q, k, v = [
        jnp.where(odd, w_buf[part, :, HS:].astype(F32), w_buf[part, :, :HS].astype(F32)) for part in range(3)
    ]
    weights_ref[:HS, :] = jnp.concatenate([q, k], axis=1).astype(BF16)
    weights_ref[HS:QKV, :] = jnp.concatenate([v[:HALF], v[HALF:]], axis=1).astype(BF16)
    load_out.wait()
    for a in range(D // BLOCK):
        weights_ref[QKV + a * HS : QKV + (a + 1) * HS, :] = wo_buf[:, a * BLOCK : (a + 1) * BLOCK]


def pack(slots, frames, targets, index, w_qkv, w_out):
    return call(
        pack_kernel,
        "pack",
        1,
        [((COPIES, ROWS, D + KMAX + EARLY), BF16), ((ROWS, KMAX), BF16), ((QKV + HS * D // BLOCK, BLOCK), BF16)],
        [HBM] * 6,
        [VMEM, VMEM, VMEM],
        [
            pltpu.VMEM((3, HS, BLOCK), BF16),
            pltpu.VMEM((HS, D), BF16),
            pltpu.VMEM((ROWS, D), BF16),
            pltpu.VMEM((ROWS, EARLY), BF16),
            pltpu.VMEM((1, KMAX), jnp.int32),
            pltpu.VMEM((1, L), jnp.int32),
            pltpu.SemaphoreType.DMA((8,)),
        ],
    )(in_hbm(slots), in_hbm(frames), in_hbm(targets), in_hbm(index), in_hbm(w_qkv), in_hbm(w_out))


def normalize(got_ref, gain_hbm, gain_ref, sem):
    load = pltpu.make_async_copy(gain_hbm, gain_ref, sem)
    load.start()
    values = got_ref[:, :D].astype(F32)
    center = values - jnp.mean(values, axis=1, keepdims=True)
    spread = jnp.mean(center * center, axis=1, keepdims=True)
    load.wait()
    return (center * lax.rsqrt(spread + NORM_EPSILON) * gain_ref[...]).astype(BF16)


def forward_kernel(
    got_ref, w_ref, gain_hbm, targets_ref, out_ref, probs_out, pick_out, qkv_out,
    probs_ref, pick_ref, qkv_ref, wqk_ref, wv_ref, gain_ref, sems,
):
    for m in range(COPIES):
        for a in range((D - EARLY) // BLOCK):
            lanes = slice(EARLY + a * BLOCK, EARLY + (a + 1) * BLOCK)
            out_ref[m, HS + a * ROWS : HS + (a + 1) * ROWS, :] = targets_ref[0, :, lanes]
    normed = normalize(got_ref, gain_hbm, gain_ref, sems.at[3 * COPIES // GROUP])
    x = lax.axis_index("x")
    for c in range(CLIPS):
        block = w_ref[c % 2, lax.rem(x + XS - c // (2 * YS), XS), c // 2 % YS]
        wqk_ref[c * HS : (c + 1) * HS, :] = block[:HS]
        wv_ref[c * HS : c * HS + HALF, :] = block[HS:, :HS]
        wv_ref[c * HS + HALF : (c + 1) * HS, :] = block[HS:, HS:]
    qk = mm(normed, wqk_ref[...]).astype(BF16).astype(F32)
    v = mm(normed, wv_ref[...]).astype(BF16).astype(F32)
    qk_t = qk.T
    qkv_t = jnp.concatenate([qk_t[:HS] * SCORE_SCALE, qk_t[HS:], v.T], axis=0).astype(BF16)
    rows = frame_ids(KMAX)
    first = lax.broadcasted_iota(jnp.int32, (EXTRA, KMAX), 0) == 0
    one_row = jnp.where(first, 1.0, 0.0).astype(BF16)
    saves = []
    for begin in range(0, COPIES, GROUP):
        group = range(begin, begin + GROUP)
        index = [got_ref[m * ROWS : (m + 1) * ROWS, D : D + KMAX].astype(F32)[:1] for m in group]
        pick = [jnp.where(rows == i, 1.0, 0.0).astype(BF16) for i in index]
        for m, p in zip(group, pick):
            pick_ref[:, m * KMAX : (m + 1) * KMAX] = p
        qkv = [mm(qkv_t, p).astype(BF16) for p in pick]
        for m, a in zip(group, qkv):
            qkv_ref[m] = a
        bias = [jnp.where(first & (i > L - 0.5), MASKED_SCORE, 0.0).astype(BF16) for i in index]
        queries = [jnp.concatenate([a[:HS], one_row], axis=0) for a in qkv]
        keys = [jnp.concatenate([a[HS : 2 * HS], e], axis=0).T for a, e in zip(qkv, bias)]
        scores = [mm(k, q) for k, q in zip(keys, queries)]
        raised = [jnp.exp(a - jnp.max(a, axis=0, keepdims=True)) for a in scores]
        probs = [a * (1.0 / jnp.sum(a, axis=0, keepdims=True)) for a in raised]
        for m, p in zip(group, probs):
            probs_ref[m] = p
        ctx = [mm(a[2 * HS :], p.astype(BF16)) for a, p in zip(qkv, probs)]
        for m, a in zip(group, ctx):
            out_ref[m, :HS, :] = a.astype(BF16)
        part = pl.ds(begin, GROUP)
        lanes = pl.ds(begin * KMAX, GROUP * KMAX)
        for here, there in (
            (probs_ref.at[part], probs_out.at[part]),
            (qkv_ref.at[part], qkv_out.at[part]),
            (pick_ref.at[:, lanes], pick_out.at[:, lanes]),
        ):
            saves.append(pltpu.make_async_copy(here, there, sems.at[len(saves)]))
            saves[-1].start()
    for save in saves:
        save.wait()


def forward(got, weights, gain, targets):
    return call(
        forward_kernel,
        "forward",
        0.1,
        [
            ((COPIES, HS + LATE, KMAX), BF16),
            ((COPIES, KMAX, KMAX), F32),
            ((L, QALL), BF16),
            ((COPIES, 3 * HS, KMAX), BF16),
        ],
        [VMEM, VMEM, HBM, VMEM],
        [VMEM, HBM, HBM, HBM],
        [
            pltpu.VMEM((COPIES, KMAX, KMAX), F32),
            pltpu.VMEM((L, QALL), BF16),
            pltpu.VMEM((COPIES, 3 * HS, KMAX), BF16),
            pltpu.VMEM((D, 2 * HS), BF16),
            pltpu.VMEM((D, HS), BF16),
            pltpu.VMEM((1, D), F32),
            pltpu.SemaphoreType.DMA((3 * COPIES // GROUP + 1,)),
        ],
    )(got, weights, in_hbm(gain), targets)


def prepare_kernel(got_ref, gain_hbm, out_ref, buf, gain_ref, sems):
    buf[...] = normalize(got_ref, gain_hbm, gain_ref, sems.at[1]).T
    save = pltpu.make_async_copy(buf, out_ref, sems.at[0])
    save.start()
    save.wait()


def prepare(got, gain):
    return call(
        prepare_kernel,
        "prepare",
        2,
        [((D, L), BF16)],
        [VMEM, HBM],
        [HBM],
        [pltpu.VMEM((D, L), BF16), pltpu.VMEM((1, D), F32), pltpu.SemaphoreType.DMA((2,))],
    )(got, in_hbm(gain))[0]


def decoder_kernel(
    recv_ref, got_ref, index_ref, embed_ref, taps_ref, *refs
):
    w_refs = refs[: 2 * XS]
    encoded_ref, dctx_ref, ctx_out, denc_out, share_out = refs[2 * XS : 2 * XS + 5]
    ctx_ref, denc_ref, share_ref, field_ref, error_ref, dfilled_ref, sems = refs[2 * XS + 5 :]
    chunks = D // LANES
    core, x = lax.axis_index("core"), lax.axis_index("x")
    parts = []
    for s in range(XS):
        chip = YS * lax.rem(x + XS - s, XS)
        slots = [side * ZS + chip + t for side in (core, 1 - core) for t in range(YS)]
        weights = [
            jnp.concatenate(
                [w_refs[s][:, a].reshape(YS * HS, BLOCK), w_refs[XS + s][:, a].reshape(YS * HS, BLOCK)], axis=0
            )
            for a in range(D // BLOCK)
        ]
        parts.append((slots, weights))
    rows = lax.broadcasted_iota(jnp.int32, (L, KMAX), 0).astype(F32)
    hit = jnp.where(rows == index_ref[...].astype(F32)[:1], 1.0, 0.0)
    masked = 1.0 - jnp.sum(hit, axis=1, keepdims=True)
    place = hit.astype(BF16)
    hit = hit.T
    live = jnp.sum(hit, axis=1, keepdims=True) > 0.5
    pick = hit.astype(BF16)
    gather = jnp.where(frame_ids(KMAX) == index_ref[...].astype(F32)[:1], 1.0, 0.0).T.astype(BF16)
    ctx_ref[...] = recv_ref[:, :HS, :]
    saves = [
        pltpu.make_async_copy(here, there, sems.at[at])
        for at, (here, there) in enumerate(
            ((ctx_ref, ctx_out), (denc_ref, denc_out), (share_ref, share_out))
        )
    ]
    saves[0].start()
    ctx = [
        jnp.concatenate([ctx_ref[at] for at in slots], axis=0).T for slots, weights in parts
    ]
    for i in range(CLIPS // 2):
        share_ref[i, :HS, :] = ctx_ref[(1 - core) * ZS + i]
    reach = KW // 2
    blocks = D // BLOCK
    for ref in (field_ref, error_ref):
        ref[:PAD] = jnp.zeros((PAD, D), F32)
        ref[PAD + L :] = jnp.zeros((PAD, D), F32)
    inside = slice(PAD, PAD + L)
    columns = [slice(c * LANES, (c + 1) * LANES) for c in range(chunks)]
    inputs = [mm(gather, got_ref[:, lanes]) for lanes in columns]
    per = LANES // BLOCK
    mixed = inputs
    for left, (slots, weights) in zip(ctx, parts):
        wide = [
            jnp.concatenate(weights[c * per : (c + 1) * per], axis=1) for c in range(chunks)
        ]
        mixed = [m + mm(left, w) for m, w in zip(mixed, wide)]
    encoded = [jnp.where(live, m, 0.0).astype(BF16) for m in mixed]
    for lanes, e in zip(columns, encoded):
        encoded_ref[:, lanes] = e
    for lanes, e in zip(columns, encoded):
        field_ref[inside, lanes] = mm(place, e) + masked * embed_ref[:, lanes].astype(F32)
    for a in range(blocks):
        lanes = slice(a * BLOCK, (a + 1) * BLOCK)
        predicted = taps_ref[:1, lanes] * field_ref[PAD - reach : PAD - reach + L, lanes]
        for t in range(1, KW):
            begin = PAD - reach + t
            predicted = predicted + taps_ref[t : t + 1, lanes] * field_ref[begin : begin + L, lanes]
        if (a + 1) * BLOCK <= EARLY:
            begin = D + KMAX + a * BLOCK
            wanted = in_order(lambda p: got_ref[p * ROWS : (p + 1) * ROWS, begin : begin + BLOCK])
        else:
            begin = HS + (a * BLOCK - EARLY) // BLOCK * ROWS
            wanted = in_order(lambda p: recv_ref[p, begin : begin + ROWS, :])
        error_ref[inside, lanes] = masked * (predicted - wanted.astype(F32)) * LOSS_SCALE
    for a in range(blocks):
        lanes = slice(a * BLOCK, (a + 1) * BLOCK)
        dfilled = taps_ref[:1, lanes] * error_ref[PAD + reach : PAD + reach + L, lanes]
        for t in range(1, KW):
            begin = PAD + reach - t
            dfilled = dfilled + taps_ref[t : t + 1, lanes] * error_ref[begin : begin + L, lanes]
        dfilled_ref[:, lanes] = dfilled.astype(BF16)
    denc = [mm(pick, dfilled_ref[:, lanes]).astype(BF16) for lanes in columns]
    for c in range(chunks):
        denc_ref[:, columns[c]] = denc[c]
        for i in range(per):
            share_ref[c * per + i, HS:, :] = denc[c][:, i * BLOCK : (i + 1) * BLOCK]
    saves[1].start()
    saves[2].start()
    denc = denc_ref[...]
    for slots, weights in parts:
        dctx = mm_nt(jnp.concatenate(weights, axis=1), denc).astype(BF16)
        for r, at in enumerate(slots):
            dctx_ref[at] = dctx[r * HS : (r + 1) * HS]
    for save in saves:
        save.wait()


def decoder(recv, got, w_out, index, embed, taps):
    return call(
        decoder_kernel,
        "decoder",
        5,
        [
            ((KMAX, D), BF16),
            ((H, HS, KMAX), BF16),
            ((H, HS, KMAX), BF16),
            ((KMAX, D), BF16),
            ((CLIPS // 2, HS + KMAX, KMAX), BF16),
        ],
        [VMEM] * (5 + 2 * XS),
        [VMEM] * 2 + [HBM] * 3,
        [
            pltpu.VMEM((H, HS, KMAX), BF16),
            pltpu.VMEM((KMAX, D), BF16),
            pltpu.VMEM((CLIPS // 2, HS + KMAX, KMAX), BF16),
            pltpu.VMEM((L + 2 * PAD, D), F32),
            pltpu.VMEM((L + 2 * PAD, D), F32),
            pltpu.VMEM((L, D), BF16),
            pltpu.SemaphoreType.DMA((3,)),
        ],
    )(recv, got, index, embed, taps, *w_out)


def out_grad_kernel(ctx_ref, denc_ref, share_ref, *refs):
    outs, both_ref = refs[:XS], refs[XS]
    core, x, y = lax.axis_index("core"), lax.axis_index("x"), lax.axis_index("y_lo")
    for a in range(D // BLOCK):
        lanes = slice(a * BLOCK, (a + 1) * BLOCK)
        both_ref[:KMAX, lanes] = denc_ref[:, lanes]
        both_ref[KMAX:, lanes] = share_ref[a, HS:, :]
    for r in range(XS):
        for s in range(YS):
            chip = YS * lax.rem(x + r, XS) + lax.rem(y + s, YS)
            left = jnp.concatenate([ctx_ref[core * ZS + chip], share_ref[chip, :HS, :]], axis=1)
            block = mm(left, both_ref[...])
            upper, lower = block[:HALF], block[HALF:]
            for a in range(D // BLOCK):
                lanes = slice(a * BLOCK, (a + 1) * BLOCK)
                first, second = upper[:, lanes], lower[:, lanes]
                even = jnp.concatenate([first[:, :HS], second[:, :HS]], axis=1)
                odd = jnp.concatenate([first[:, HS:], second[:, HS:]], axis=1)
                outs[r][s, slot(2 * a)] = even.astype(BF16)
                outs[r][s, slot(2 * a + 1)] = odd.astype(BF16)


def out_grad(ctx, denc, share):
    return call(
        out_grad_kernel,
        "out_grad",
        1,
        [((YS, COPIES, HALF, BLOCK), BF16)] * XS,
        [VMEM] * 3,
        [VMEM] * XS,
        [pltpu.VMEM((2 * KMAX, D), BF16)],
    )(ctx, denc, share)


def backward_kernel(
    dctx_ref, probs_hbm, pick_hbm, qkv_hbm, normed_hbm, out_ref,
    probs_ref, pick_ref, qkv_ref, normed_ref, dqkv_ref, sems,
):
    loads = []
    for at, (there, here) in enumerate(
        ((qkv_hbm, qkv_ref), (probs_hbm, probs_ref), (pick_hbm, pick_ref), (normed_hbm, normed_ref))
    ):
        loads.append(pltpu.make_async_copy(there, here, sems.at[at]))
        loads[at].start()
    loads[0].wait()
    loads[1].wait()
    for begin in range(0, COPIES, GROUP):
        group = range(begin, begin + GROUP)
        dctx = [dctx_ref[m] for m in group]
        qkv = [qkv_ref[m] for m in group]
        probs = [probs_ref[m] for m in group]
        dprobs = [mm(a[2 * HS :].T, d) for a, d in zip(qkv, dctx)]
        along = [jnp.sum(p * d, axis=0, keepdims=True) for p, d in zip(probs, dprobs)]
        dscores = [(p * (d - a)).astype(BF16) for p, d, a in zip(probs, dprobs, along)]
        dvalue = [mm(p.astype(BF16), d.T) for p, d in zip(probs, dctx)]
        dkey = [mm(d, a[:HS].T) for d, a in zip(dscores, qkv)]
        dquery = [(mm(a[HS : 2 * HS], d) * SCORE_SCALE).T for a, d in zip(qkv, dscores)]
        for m, q, k, v in zip(group, dquery, dkey, dvalue):
            dqkv = jnp.concatenate([q, k, v], axis=1)
            dqkv_ref[m * KMAX : (m + 1) * KMAX, :] = dqkv.astype(BF16)
    loads[2].wait()
    loads[3].wait()
    total = mm(pick_ref[...], dqkv_ref[...]).astype(BF16)
    grad = mm(normed_ref[...], total).astype(BF16)
    for c in range(CLIPS):
        block = grad[c * HS : (c + 1) * HS]
        out_ref[c, :HS, :] = block[:, : 2 * HS]
        out_ref[c, HS:, :HS] = block[:HALF, 2 * HS :]
        out_ref[c, HS:, HS:] = block[HALF:, 2 * HS :]


def backward(dctx, probs, pick, qkv, normed):
    return call(
        backward_kernel,
        "backward",
        5,
        [((CLIPS, HS + HALF, BLOCK), BF16)],
        [VMEM] + [HBM] * 4,
        [VMEM],
        [
            pltpu.VMEM((COPIES, KMAX, KMAX), F32),
            pltpu.VMEM((L, QALL), BF16),
            pltpu.VMEM((COPIES, 3 * HS, KMAX), BF16),
            pltpu.VMEM((D, L), BF16),
            pltpu.VMEM((QALL, 3 * HS), BF16),
            pltpu.SemaphoreType.DMA((4,)),
        ],
    )(dctx, in_hbm(probs), in_hbm(pick), in_hbm(qkv), in_hbm(normed))[0]


def collect_kernel(terms_ref, mine_ref, other_ref, out_ref):
    head = head_here()
    out_ref[:, :HALF, :] = (mine_ref[...].astype(F32) + other_ref[...].astype(F32)).astype(BF16)
    out_ref[:, HALF:, :] = jnp.zeros((COPIES, HALF, BLOCK), BF16)
    term = jnp.sum(terms_ref[...].astype(F32), axis=0)
    upper, lower = term[:HALF], term[HALF:HS]
    query = jnp.concatenate([upper[:, :HS], lower[:, :HS]], axis=1)
    key = jnp.concatenate([upper[:, HS:], lower[:, HS:]], axis=1)
    for part, piece in enumerate((query, key, term[HS:])):
        out_ref[slot((part * H + head) // 3), HALF:, :] = piece.astype(BF16)


def collect(terms, mine, other):
    return call(
        collect_kernel,
        "collect",
        1,
        [((COPIES, HS, BLOCK), BF16)],
        [VMEM] * 3,
        [VMEM],
    )(terms, mine, other)[0]


def emit_kernel(source_hbm, out_ref, buf, sem):
    load = pltpu.make_async_copy(source_hbm, buf, sem)
    load.start()
    load.wait()
    out_ref[...] = buf[...]


def emit(encoded):
    return call(
        emit_kernel,
        "emit",
        5,
        [((KMAX, D), BF16)],
        [HBM],
        [VMEM],
        [pltpu.VMEM((KMAX, D), BF16), pltpu.SemaphoreType.DMA(())],
    )(in_hbm(encoded))[0]


def finish_kernel(last_ref, qkv_ref, out_ref):
    total = jnp.sum(last_ref[:, :HALF, :].astype(F32), axis=0)
    out_ref[:HALF, :] = total[:, :HS]
    out_ref[HALF:, :] = total[:, HS:]
    for i in range(3):
        block = last_ref[slot(lax.rem(3 * head_here() + i, COPIES)), HALF:, :].astype(F32)
        qkv_ref[:HALF, i * HS : (i + 1) * HS] = block[:, :HS]
        qkv_ref[HALF:, i * HS : (i + 1) * HS] = block[:, HS:]


def finish(last):
    return call(
        finish_kernel,
        "finish",
        1,
        [((HS, 3 * HS), F32), ((HS, HS), F32)],
        [VMEM],
        [VMEM] * 2,
    )(last)


def swap(array, axes):
    return lax.all_to_all(array, axes, 0, 0, tiled=True)


def total(*parts):
    result = parts[0].astype(F32)
    for part in parts[1:]:
        result = result + part.astype(F32)
    return result.astype(BF16)


def per_device(
    frames,
    targets,
    kept_index,
    kept_count,
    fill_slot,
    norm_gain,
    w_qkv,
    w_out,
    mask_embed,
    dec_kernel,
):
    gain = norm_gain[None, :]
    sent, index, weights = pack(fill_slot, frames, targets, kept_index, w_qkv, w_out)
    got = swap(sent, RING).reshape(L, D + KMAX + EARLY)
    weights = lax.all_gather(weights, "y_lo", axis=0)
    near = weights[:, QKV:].reshape(YS, D // BLOCK, HS, BLOCK)
    weights = weights[:, :QKV]
    around = [weights] + [
        lax.ppermute(weights, "x", [(i, (i + r) % XS) for i in range(XS)]) for r in range(1, XS)
    ]
    weights = lax.all_gather(jnp.stack(around), "core", axis=0)

    sent, probs, pick, qkv = forward(got, weights, gain, targets)
    normed = prepare(got, gain)
    recv = swap(sent, RING)
    near, sent = lax.optimization_barrier((near, sent))
    w_out = [near]
    for r in range(1, XS):
        w_out.append(lax.ppermute(near, "x", [(i, (i + r) % XS) for i in range(XS)]))
    w_out += [lax.ppermute(part, "core", [(0, 1), (1, 0)]) for part in w_out]
    encoded, dctx, ctx, denc, share = decoder(
        recv, got, w_out, index, mask_embed[None, :], dec_kernel
    )
    dctx = swap(dctx, RING)

    share = lax.ppermute(share, "core", [(0, 1), (1, 0)])
    parts = list(out_grad(ctx, denc, share))
    for r in range(1, XS):
        parts[r] = lax.ppermute(parts[r], "x", [(i, (i + r) % XS) for i in range(XS)])
    mine = total(*[part[0] for part in parts])
    other = total(*[part[1] for part in parts])
    other = lax.ppermute(other, "y_lo", [(0, 1), (1, 0)])

    terms = swap(backward(dctx, probs, pick, qkv, normed), CLIP)
    grad_qkv, grad_out = finish(swap(collect(terms, mine, other), RING))
    return (emit(encoded)[None, None], grad_qkv, grad_out)


def solution(mesh):
    fine = Mesh(mesh.devices.reshape(XS, YS, 2, 8, 2), ("x", "y_lo", "core", "z", "y_hi"))
    in_specs = (
        P(CLIP, COPY, None),
        P(CLIP, COPY, None),
        P(CLIP, COPY, None),
        P(CLIP, COPY),
        P(CLIP, COPY, None),
        P(),
        P(CLIP, None),
        P(CLIP, None),
        P(),
        P(),
    )
    out_specs = (P(CLIP, COPY, None, None), P(CLIP, COPY), P(CLIP, COPY))
    return jax.shard_map(
        per_device, mesh=fine, in_specs=in_specs, out_specs=out_specs, check_vma=False
    )
```

```python
import jax
import jax.numpy as jnp
from jax import lax
from jax.experimental import pallas as pl
from jax.experimental.pallas import tpu as pltpu
from jax.sharding import Mesh
from jax.sharding import PartitionSpec as P


D = 1024
H = 16
HS = 64
HALF = HS // 2
L = 256
KMAX = 128
KW = 7
CLIPS = 16
COPIES = 16
QALL = COPIES * KMAX
NORM_EPSILON = 1e-05
MASKED_SCORE = -1e30
SCORE_SCALE = HS**-0.5
ROWS = L // COPIES
LOSS_SCALE = (KMAX * CLIPS * COPIES) ** -0.5
PAD = 8
LANES = 256
BLOCK = 128
EARLY = D // 4
LATE = (D - EARLY) // BLOCK * ROWS
QKV = HS + HALF
EXTRA = 16
GROUP = 8
VMEM_LIMIT = 20 * 1024 * 1024

XS, YS = 4, 2
CLIP = ("x", "y_lo", "core")
COPY = ("z", "y_hi")
RING = ("y_hi", "z")
ZS, ZY = 8, 2
F32 = jnp.float32
BF16 = jnp.bfloat16

VMEM = pl.BlockSpec(memory_space=pltpu.VMEM)
HBM = pl.BlockSpec(memory_space=pltpu.HBM)


def slot(copy):
    return copy % ZY * ZS + copy // ZY


def copy_of(place):
    return place % ZS * ZY + place // ZS


def in_order(blocks):
    return jnp.concatenate([blocks(slot(copy)) for copy in range(COPIES)], axis=0)


def frame_ids(width):
    row = lax.broadcasted_iota(jnp.int32, (L, width), 0)
    return (copy_of(row // ROWS) * ROWS + row % ROWS).astype(F32)


def head_here():
    return lax.axis_index("z") * ZY + lax.axis_index("y_hi")


def mm(left, right):
    return jnp.dot(left, right, preferred_element_type=F32)


def mm_nt(left, right):
    return lax.dot_general(left, right, (((1,), (1,)), ((), ())), preferred_element_type=F32)


def call(kernel, name, microseconds, out_shape, in_specs, out_specs, scratch=()):
    return pl.pallas_call(
        kernel,
        out_shape=[
            pltpu.HBM(shape, dtype) if spec is HBM else jax.ShapeDtypeStruct(shape, dtype)
            for (shape, dtype), spec in zip(out_shape, out_specs)
        ],
        in_specs=in_specs,
        out_specs=out_specs,
        scratch_shapes=list(scratch),
        compiler_params=pltpu.CompilerParams(vmem_limit_bytes=VMEM_LIMIT),
        cost_estimate=pl.CostEstimate(
            flops=int(microseconds * 1e9), bytes_accessed=1024, transcendentals=0
        ),
        name=name,
    )


def in_hbm(array):
    return pltpu.with_memory_space_constraint(array, pltpu.HBM)


def pack_kernel(
    slots_hbm, frames_hbm, targets_hbm, index_hbm, w_ref, wo_hbm,
    sent_ref, index_out, weights_ref, w_buf, wo_buf, frames_ref, targets_ref, index_ref, slots_ref, sems,
):
    head = head_here()
    copies = []
    load_index = pltpu.make_async_copy(index_hbm.at[0], index_ref, sems.at[3])
    load_index.start()
    load_slots = pltpu.make_async_copy(slots_hbm.at[0], slots_ref, sems.at[7])
    load_slots.start()
    load_frames = pltpu.make_async_copy(frames_hbm.at[0], frames_ref, sems.at[4])
    load_frames.start()
    load_targets = pltpu.make_async_copy(targets_hbm.at[0, :, :EARLY], targets_ref, sems.at[6])
    load_targets.start()
    load_out = pltpu.make_async_copy(wo_hbm, wo_buf, sems.at[5])
    load_out.start()
    for part in range(3):
        begin = pl.multiple_of(part * D + (head // 2) * BLOCK, BLOCK)
        copies.append(
            pltpu.make_async_copy(w_ref.at[:, pl.ds(begin, BLOCK)], w_buf.at[part], sems.at[part])
        )
        copies[part].start()
    lanes = lax.broadcasted_iota(jnp.int32, (ROWS, KMAX), 1)
    load_index.wait()
    load_slots.wait()
    kept = jnp.where(slots_ref[...] < KMAX, 1.0, 0.0)
    count = jnp.sum(kept, axis=1, keepdims=True)
    index = jnp.broadcast_to(index_ref[...], (ROWS, KMAX))
    index = jnp.where(lanes.astype(F32) < count, index, L).astype(F32).astype(BF16)
    index_out[...] = index
    load_frames.wait()
    load_targets.wait()
    for m in range(COPIES):
        sent_ref[m, :, :D] = frames_ref[...]
        sent_ref[m, :, D : D + KMAX] = index
        sent_ref[m, :, D + KMAX :] = targets_ref[...]
    odd = head % 2 == 1
    for part in range(3):
        copies[part].wait()
    q, k, v = [
        jnp.where(odd, w_buf[part, :, HS:].astype(F32), w_buf[part, :, :HS].astype(F32)) for part in range(3)
    ]
    weights_ref[:HS, :] = jnp.concatenate([q, k], axis=1).astype(BF16)
    weights_ref[HS:QKV, :] = jnp.concatenate([v[:HALF], v[HALF:]], axis=1).astype(BF16)
    load_out.wait()
    for a in range(D // BLOCK):
        weights_ref[QKV + a * HS : QKV + (a + 1) * HS, :] = wo_buf[:, a * BLOCK : (a + 1) * BLOCK]


def pack(slots, frames, targets, index, w_qkv, w_out):
    return call(
        pack_kernel,
        "pack",
        1,
        [((COPIES, ROWS, D + KMAX + EARLY), BF16), ((ROWS, KMAX), BF16), ((QKV + HS * D // BLOCK, BLOCK), BF16)],
        [HBM] * 6,
        [VMEM, VMEM, VMEM],
        [
            pltpu.VMEM((3, HS, BLOCK), BF16),
            pltpu.VMEM((HS, D), BF16),
            pltpu.VMEM((ROWS, D), BF16),
            pltpu.VMEM((ROWS, EARLY), BF16),
            pltpu.VMEM((1, KMAX), jnp.int32),
            pltpu.VMEM((1, L), jnp.int32),
            pltpu.SemaphoreType.DMA((8,)),
        ],
    )(in_hbm(slots), in_hbm(frames), in_hbm(targets), in_hbm(index), in_hbm(w_qkv), in_hbm(w_out))


def normalize(got_ref, gain_hbm, gain_ref, sem):
    load = pltpu.make_async_copy(gain_hbm, gain_ref, sem)
    load.start()
    values = got_ref[:, :D].astype(F32)
    center = values - jnp.mean(values, axis=1, keepdims=True)
    spread = jnp.mean(center * center, axis=1, keepdims=True)
    load.wait()
    return (center * lax.rsqrt(spread + NORM_EPSILON) * gain_ref[...]).astype(BF16)


def forward_kernel(
    got_ref, w_ref, gain_hbm, targets_ref, out_ref, probs_out, pick_out, qkv_out,
    probs_ref, pick_ref, qkv_ref, wqk_ref, wv_ref, gain_ref, sems,
):
    for m in range(COPIES):
        for a in range((D - EARLY) // BLOCK):
            lanes = slice(EARLY + a * BLOCK, EARLY + (a + 1) * BLOCK)
            out_ref[m, HS + a * ROWS : HS + (a + 1) * ROWS, :] = targets_ref[0, :, lanes]
    normed = normalize(got_ref, gain_hbm, gain_ref, sems.at[3 * COPIES // GROUP])
    x = lax.axis_index("x")
    for c in range(CLIPS):
        block = w_ref[c % 2, lax.rem(x + XS - c // (2 * YS), XS), c // 2 % YS]
        wqk_ref[c * HS : (c + 1) * HS, :] = block[:HS]
        wv_ref[c * HS : c * HS + HALF, :] = block[HS:, :HS]
        wv_ref[c * HS + HALF : (c + 1) * HS, :] = block[HS:, HS:]
    qk = mm(normed, wqk_ref[...]).astype(BF16).astype(F32)
    v = mm(normed, wv_ref[...]).astype(BF16).astype(F32)
    qk_t = qk.T
    qkv_t = jnp.concatenate([qk_t[:HS] * SCORE_SCALE, qk_t[HS:], v.T], axis=0).astype(BF16)
    rows = frame_ids(KMAX)
    first = lax.broadcasted_iota(jnp.int32, (EXTRA, KMAX), 0) == 0
    one_row = jnp.where(first, 1.0, 0.0).astype(BF16)
    saves = []

    def save(here, there):
        saves.append(pltpu.make_async_copy(here, there, sems.at[len(saves)]))
        saves[-1].start()

    for begin in range(0, COPIES, GROUP):
        group = range(begin, begin + GROUP)
        index = [got_ref[m * ROWS : (m + 1) * ROWS, D : D + KMAX].astype(F32)[:1] for m in group]
        pick = [jnp.where(rows == i, 1.0, 0.0).astype(BF16) for i in index]
        for m, p in zip(group, pick):
            pick_ref[:, m * KMAX : (m + 1) * KMAX] = p
        qkv = [mm(qkv_t, p).astype(BF16) for p in pick]
        for m, a in zip(group, qkv):
            qkv_ref[m] = a
        part = pl.ds(begin, GROUP)
        lanes = pl.ds(begin * KMAX, GROUP * KMAX)
        save(pick_ref.at[:, lanes], pick_out.at[:, lanes])
        save(qkv_ref.at[part], qkv_out.at[part])
        bias = [jnp.where(first & (i > L - 0.5), MASKED_SCORE, 0.0).astype(BF16) for i in index]
        queries = [jnp.concatenate([a[:HS], one_row], axis=0) for a in qkv]
        keys = [jnp.concatenate([a[HS : 2 * HS], e], axis=0).T for a, e in zip(qkv, bias)]
        scores = [mm(k, q) for k, q in zip(keys, queries)]
        raised = [jnp.exp(a - jnp.max(a, axis=0, keepdims=True)) for a in scores]
        probs = [a * (1.0 / jnp.sum(a, axis=0, keepdims=True)) for a in raised]
        for m, p in zip(group, probs):
            probs_ref[m] = p
        ctx = [mm(a[2 * HS :], p.astype(BF16)) for a, p in zip(qkv, probs)]
        for m, a in zip(group, ctx):
            out_ref[m, :HS, :] = a.astype(BF16)
        save(probs_ref.at[part], probs_out.at[part])
    for copy in saves:
        copy.wait()


def forward(got, weights, gain, targets):
    return call(
        forward_kernel,
        "forward",
        0.1,
        [
            ((COPIES, HS + LATE, KMAX), BF16),
            ((COPIES, KMAX, KMAX), F32),
            ((L, QALL), BF16),
            ((COPIES, 3 * HS, KMAX), BF16),
        ],
        [VMEM, VMEM, HBM, VMEM],
        [VMEM, HBM, HBM, HBM],
        [
            pltpu.VMEM((COPIES, KMAX, KMAX), F32),
            pltpu.VMEM((L, QALL), BF16),
            pltpu.VMEM((COPIES, 3 * HS, KMAX), BF16),
            pltpu.VMEM((D, 2 * HS), BF16),
            pltpu.VMEM((D, HS), BF16),
            pltpu.VMEM((1, D), F32),
            pltpu.SemaphoreType.DMA((3 * COPIES // GROUP + 1,)),
        ],
    )(got, weights, in_hbm(gain), targets)


def prepare_kernel(got_ref, gain_hbm, out_ref, buf, gain_ref, sems):
    buf[...] = normalize(got_ref, gain_hbm, gain_ref, sems.at[1]).T
    save = pltpu.make_async_copy(buf, out_ref, sems.at[0])
    save.start()
    save.wait()


def prepare(got, gain):
    return call(
        prepare_kernel,
        "prepare",
        2,
        [((D, L), BF16)],
        [VMEM, HBM],
        [HBM],
        [pltpu.VMEM((D, L), BF16), pltpu.VMEM((1, D), F32), pltpu.SemaphoreType.DMA((2,))],
    )(got, in_hbm(gain))[0]


def decoder_kernel(
    recv_ref, got_ref, index_ref, embed_ref, taps_ref, *refs
):
    w_refs = refs[: 2 * XS]
    encoded_out, dctx_out, ctx_out, denc_out, share_out = refs[2 * XS : 2 * XS + 5]
    encoded_ref, dctx_ref, ctx_ref, denc_ref, share_ref, field_ref, error_ref, dfilled_ref, sems = refs[2 * XS + 5 :]
    chunks = D // LANES
    core, x = lax.axis_index("core"), lax.axis_index("x")
    parts = []
    for s in range(XS):
        chip = YS * lax.rem(x + XS - s, XS)
        slots = [side * ZS + chip + t for side in (core, 1 - core) for t in range(YS)]
        weights = [
            jnp.concatenate(
                [w_refs[s][:, a].reshape(YS * HS, BLOCK), w_refs[XS + s][:, a].reshape(YS * HS, BLOCK)], axis=0
            )
            for a in range(D // BLOCK)
        ]
        parts.append((slots, weights))
    rows = lax.broadcasted_iota(jnp.int32, (L, KMAX), 0).astype(F32)
    hit = jnp.where(rows == index_ref[...].astype(F32)[:1], 1.0, 0.0)
    masked = 1.0 - jnp.sum(hit, axis=1, keepdims=True)
    place = hit.astype(BF16)
    hit = hit.T
    live = jnp.sum(hit, axis=1, keepdims=True) > 0.5
    pick = hit.astype(BF16)
    gather = jnp.where(frame_ids(KMAX) == index_ref[...].astype(F32)[:1], 1.0, 0.0).T.astype(BF16)
    ctx_ref[...] = recv_ref[:, :HS, :]
    saves = [
        pltpu.make_async_copy(here, there, sems.at[at])
        for at, (here, there) in enumerate(
            ((ctx_ref, ctx_out), (denc_ref, denc_out), (share_ref, share_out), (encoded_ref, encoded_out))
        )
    ]
    saves[0].start()
    ctx = [
        jnp.concatenate([ctx_ref[at] for at in slots], axis=0).T for slots, weights in parts
    ]
    for i in range(CLIPS // 2):
        share_ref[i, :HS, :] = ctx_ref[(1 - core) * ZS + i]
    reach = KW // 2
    blocks = D // BLOCK
    for ref in (field_ref, error_ref):
        ref[:PAD] = jnp.zeros((PAD, D), F32)
        ref[PAD + L :] = jnp.zeros((PAD, D), F32)
    inside = slice(PAD, PAD + L)
    columns = [slice(c * LANES, (c + 1) * LANES) for c in range(chunks)]
    inputs = [mm(gather, got_ref[:, lanes]) for lanes in columns]
    per = LANES // BLOCK
    mixed = inputs
    for left, (slots, weights) in zip(ctx, parts):
        wide = [
            jnp.concatenate(weights[c * per : (c + 1) * per], axis=1) for c in range(chunks)
        ]
        mixed = [m + mm(left, w) for m, w in zip(mixed, wide)]
    encoded = [jnp.where(live, m, 0.0).astype(BF16) for m in mixed]
    for lanes, e in zip(columns, encoded):
        encoded_ref[:, lanes] = e
    saves[3].start()
    for lanes, e in zip(columns, encoded):
        field_ref[inside, lanes] = mm(place, e) + masked * embed_ref[:, lanes].astype(F32)
    for a in range(blocks):
        lanes = slice(a * BLOCK, (a + 1) * BLOCK)
        predicted = taps_ref[:1, lanes] * field_ref[PAD - reach : PAD - reach + L, lanes]
        for t in range(1, KW):
            begin = PAD - reach + t
            predicted = predicted + taps_ref[t : t + 1, lanes] * field_ref[begin : begin + L, lanes]
        if (a + 1) * BLOCK <= EARLY:
            begin = D + KMAX + a * BLOCK
            wanted = in_order(lambda p: got_ref[p * ROWS : (p + 1) * ROWS, begin : begin + BLOCK])
        else:
            begin = HS + (a * BLOCK - EARLY) // BLOCK * ROWS
            wanted = in_order(lambda p: recv_ref[p, begin : begin + ROWS, :])
        error_ref[inside, lanes] = masked * (predicted - wanted.astype(F32)) * LOSS_SCALE
    for a in range(blocks):
        lanes = slice(a * BLOCK, (a + 1) * BLOCK)
        dfilled = taps_ref[:1, lanes] * error_ref[PAD + reach : PAD + reach + L, lanes]
        for t in range(1, KW):
            begin = PAD + reach - t
            dfilled = dfilled + taps_ref[t : t + 1, lanes] * error_ref[begin : begin + L, lanes]
        dfilled_ref[:, lanes] = dfilled.astype(BF16)
    denc = [mm(pick, dfilled_ref[:, lanes]).astype(BF16) for lanes in columns]
    for c in range(chunks):
        denc_ref[:, columns[c]] = denc[c]
        for i in range(per):
            share_ref[c * per + i, HS:, :] = denc[c][:, i * BLOCK : (i + 1) * BLOCK]
    saves[1].start()
    saves[2].start()
    denc = denc_ref[...]
    for slots, weights in parts:
        dctx = mm_nt(jnp.concatenate(weights, axis=1), denc).astype(BF16)
        for r, at in enumerate(slots):
            dctx_ref[at] = dctx[r * HS : (r + 1) * HS]
            saves.append(pltpu.make_async_copy(dctx_ref.at[at], dctx_out.at[at], sems.at[len(saves)]))
            saves[-1].start()
    for save in saves:
        save.wait()


def decoder(recv, got, w_out, index, embed, taps):
    return call(
        decoder_kernel,
        "decoder",
        5,
        [
            ((KMAX, D), BF16),
            ((H, HS, KMAX), BF16),
            ((H, HS, KMAX), BF16),
            ((KMAX, D), BF16),
            ((CLIPS // 2, HS + KMAX, KMAX), BF16),
        ],
        [VMEM] * (5 + 2 * XS),
        [HBM] * 5,
        [
            pltpu.VMEM((KMAX, D), BF16),
            pltpu.VMEM((H, HS, KMAX), BF16),
            pltpu.VMEM((H, HS, KMAX), BF16),
            pltpu.VMEM((KMAX, D), BF16),
            pltpu.VMEM((CLIPS // 2, HS + KMAX, KMAX), BF16),
            pltpu.VMEM((L + 2 * PAD, D), F32),
            pltpu.VMEM((L + 2 * PAD, D), F32),
            pltpu.VMEM((L, D), BF16),
            pltpu.SemaphoreType.DMA((4 + H,)),
        ],
    )(recv, got, index, embed, taps, *w_out)


def out_grad_kernel(ctx_ref, denc_ref, share_ref, *refs):
    outs, both_ref = refs[:XS], refs[XS]
    core, x, y = lax.axis_index("core"), lax.axis_index("x"), lax.axis_index("y_lo")
    for a in range(D // BLOCK):
        lanes = slice(a * BLOCK, (a + 1) * BLOCK)
        both_ref[:KMAX, lanes] = denc_ref[:, lanes]
        both_ref[KMAX:, lanes] = share_ref[a, HS:, :]
    for r in range(XS):
        for s in range(YS):
            chip = YS * lax.rem(x + r, XS) + lax.rem(y + s, YS)
            left = jnp.concatenate([ctx_ref[core * ZS + chip], share_ref[chip, :HS, :]], axis=1)
            block = mm(left, both_ref[...])
            upper, lower = block[:HALF], block[HALF:]
            for a in range(D // BLOCK):
                lanes = slice(a * BLOCK, (a + 1) * BLOCK)
                first, second = upper[:, lanes], lower[:, lanes]
                even = jnp.concatenate([first[:, :HS], second[:, :HS]], axis=1)
                odd = jnp.concatenate([first[:, HS:], second[:, HS:]], axis=1)
                outs[r][s, slot(2 * a)] = even.astype(BF16)
                outs[r][s, slot(2 * a + 1)] = odd.astype(BF16)


def out_grad(ctx, denc, share):
    return call(
        out_grad_kernel,
        "out_grad",
        1,
        [((YS, COPIES, HALF, BLOCK), BF16)] * XS,
        [VMEM] * 3,
        [VMEM] * XS,
        [pltpu.VMEM((2 * KMAX, D), BF16)],
    )(ctx, denc, share)


def backward_kernel(
    dctx_ref, probs_ref, pick_hbm, qkv_ref, normed_hbm, out_ref, pick_ref, normed_ref, dqkv_ref, sems
):
    loads = []
    for at, (there, here) in enumerate(((pick_hbm, pick_ref), (normed_hbm, normed_ref))):
        loads.append(pltpu.make_async_copy(there, here, sems.at[at]))
        loads[at].start()
    for begin in range(0, COPIES, GROUP):
        group = range(begin, begin + GROUP)
        dctx = [dctx_ref[m] for m in group]
        qkv = [qkv_ref[m] for m in group]
        probs = [probs_ref[m] for m in group]
        dprobs = [mm(a[2 * HS :].T, d) for a, d in zip(qkv, dctx)]
        along = [jnp.sum(p * d, axis=0, keepdims=True) for p, d in zip(probs, dprobs)]
        dscores = [(p * (d - a)).astype(BF16) for p, d, a in zip(probs, dprobs, along)]
        dvalue = [mm(p.astype(BF16), d.T) for p, d in zip(probs, dctx)]
        dkey = [mm(d, a[:HS].T) for d, a in zip(dscores, qkv)]
        dquery = [(mm(a[HS : 2 * HS], d) * SCORE_SCALE).T for a, d in zip(qkv, dscores)]
        for m, q, k, v in zip(group, dquery, dkey, dvalue):
            dqkv = jnp.concatenate([q, k, v], axis=1)
            dqkv_ref[m * KMAX : (m + 1) * KMAX, :] = dqkv.astype(BF16)
    loads[0].wait()
    loads[1].wait()
    total = mm(pick_ref[...], dqkv_ref[...]).astype(BF16)
    grad = mm(normed_ref[...], total).astype(BF16)
    for c in range(CLIPS):
        block = grad[c * HS : (c + 1) * HS]
        out_ref[c, :HS, :] = block[:, : 2 * HS]
        out_ref[c, HS:, :HS] = block[:HALF, 2 * HS :]
        out_ref[c, HS:, HS:] = block[HALF:, 2 * HS :]


def backward(dctx, probs, pick, qkv, normed):
    return call(
        backward_kernel,
        "backward",
        5,
        [((CLIPS, HS + HALF, BLOCK), BF16)],
        [VMEM, VMEM, HBM, VMEM, HBM],
        [VMEM],
        [
            pltpu.VMEM((L, QALL), BF16),
            pltpu.VMEM((D, L), BF16),
            pltpu.VMEM((QALL, 3 * HS), BF16),
            pltpu.SemaphoreType.DMA((2,)),
        ],
    )(dctx, probs, in_hbm(pick), qkv, in_hbm(normed))[0]


def collect_kernel(terms_ref, mine_ref, other_ref, out_ref):
    head = head_here()
    out_ref[:, :HALF, :] = (mine_ref[...].astype(F32) + other_ref[...].astype(F32)).astype(BF16)
    out_ref[:, HALF:, :] = jnp.zeros((COPIES, HALF, BLOCK), BF16)
    term = jnp.sum(terms_ref[...].astype(F32), axis=0)
    upper, lower = term[:HALF], term[HALF:HS]
    query = jnp.concatenate([upper[:, :HS], lower[:, :HS]], axis=1)
    key = jnp.concatenate([upper[:, HS:], lower[:, HS:]], axis=1)
    for part, piece in enumerate((query, key, term[HS:])):
        out_ref[slot((part * H + head) // 3), HALF:, :] = piece.astype(BF16)


def collect(terms, mine, other):
    return call(
        collect_kernel,
        "collect",
        1,
        [((COPIES, HS, BLOCK), BF16)],
        [VMEM] * 3,
        [VMEM],
    )(terms, mine, other)[0]


def emit_kernel(source_hbm, out_ref, buf, sem):
    load = pltpu.make_async_copy(source_hbm, buf, sem)
    load.start()
    load.wait()
    out_ref[...] = buf[...]


def emit(encoded):
    return call(
        emit_kernel,
        "emit",
        5,
        [((KMAX, D), BF16)],
        [HBM],
        [VMEM],
        [pltpu.VMEM((KMAX, D), BF16), pltpu.SemaphoreType.DMA(())],
    )(in_hbm(encoded))[0]


def finish_kernel(last_ref, qkv_ref, out_ref):
    total = jnp.sum(last_ref[:, :HALF, :].astype(F32), axis=0)
    out_ref[:HALF, :] = total[:, :HS]
    out_ref[HALF:, :] = total[:, HS:]
    for i in range(3):
        block = last_ref[slot(lax.rem(3 * head_here() + i, COPIES)), HALF:, :].astype(F32)
        qkv_ref[:HALF, i * HS : (i + 1) * HS] = block[:, :HS]
        qkv_ref[HALF:, i * HS : (i + 1) * HS] = block[:, HS:]


def finish(last):
    return call(
        finish_kernel,
        "finish",
        1,
        [((HS, 3 * HS), F32), ((HS, HS), F32)],
        [VMEM],
        [VMEM] * 2,
    )(last)


def swap(array, axes):
    return lax.all_to_all(array, axes, 0, 0, tiled=True)


def total(*parts):
    result = parts[0].astype(F32)
    for part in parts[1:]:
        result = result + part.astype(F32)
    return result.astype(BF16)


def per_device(
    frames,
    targets,
    kept_index,
    kept_count,
    fill_slot,
    norm_gain,
    w_qkv,
    w_out,
    mask_embed,
    dec_kernel,
):
    gain = norm_gain[None, :]
    sent, index, weights = pack(fill_slot, frames, targets, kept_index, w_qkv, w_out)
    got = swap(sent, RING).reshape(L, D + KMAX + EARLY)
    weights = lax.all_gather(weights, "y_lo", axis=0)
    near = weights[:, QKV:].reshape(YS, D // BLOCK, HS, BLOCK)
    weights = weights[:, :QKV]
    around = [weights] + [
        lax.ppermute(weights, "x", [(i, (i + r) % XS) for i in range(XS)]) for r in range(1, XS)
    ]
    weights = lax.all_gather(jnp.stack(around), "core", axis=0)

    sent, probs, pick, qkv = forward(got, weights, gain, targets)
    normed = prepare(got, gain)
    recv = swap(sent, RING)
    near, sent = lax.optimization_barrier((near, sent))
    w_out = [near]
    for r in range(1, XS):
        w_out.append(lax.ppermute(near, "x", [(i, (i + r) % XS) for i in range(XS)]))
    w_out += [lax.ppermute(part, "core", [(0, 1), (1, 0)]) for part in w_out]
    encoded, dctx, ctx, denc, share = decoder(
        recv, got, w_out, index, mask_embed[None, :], dec_kernel
    )
    dctx = swap(dctx, RING)

    share = lax.ppermute(share, "core", [(0, 1), (1, 0)])
    parts = list(out_grad(ctx, denc, share))
    for r in range(1, XS):
        parts[r] = lax.ppermute(parts[r], "x", [(i, (i + r) % XS) for i in range(XS)])
    mine = total(*[part[0] for part in parts])
    other = total(*[part[1] for part in parts])
    other = lax.ppermute(other, "y_lo", [(0, 1), (1, 0)])

    terms = swap(backward(dctx, probs, pick, qkv, normed), CLIP)
    grad_qkv, grad_out = finish(swap(collect(terms, mine, other), RING))
    return (emit(encoded)[None, None], grad_qkv, grad_out)


def solution(mesh):
    fine = Mesh(mesh.devices.reshape(XS, YS, 2, 8, 2), ("x", "y_lo", "core", "z", "y_hi"))
    in_specs = (
        P(CLIP, COPY, None),
        P(CLIP, COPY, None),
        P(CLIP, COPY, None),
        P(CLIP, COPY),
        P(CLIP, COPY, None),
        P(),
        P(CLIP, None),
        P(CLIP, None),
        P(),
        P(),
    )
    out_specs = (P(CLIP, COPY, None, None), P(CLIP, COPY), P(CLIP, COPY))
    return jax.shard_map(
        per_device, mesh=fine, in_specs=in_specs, out_specs=out_specs, check_vma=False
    )
```

```python
import jax
import jax.numpy as jnp
from jax import lax
from jax.experimental import pallas as pl
from jax.experimental.pallas import tpu as pltpu
from jax.sharding import Mesh
from jax.sharding import PartitionSpec as P


D = 1024
H = 16
HS = 64
HALF = HS // 2
L = 256
KMAX = 128
KW = 7
CLIPS = 16
COPIES = 16
QALL = COPIES * KMAX
NORM_EPSILON = 1e-05
MASKED_SCORE = -1e30
SCORE_SCALE = HS**-0.5
ROWS = L // COPIES
LOSS_SCALE = (KMAX * CLIPS * COPIES) ** -0.5
PAD = 8
LANES = 256
BLOCK = 128
EARLY = D // 4
LATE = (D - EARLY) // BLOCK * ROWS
QKV = HS + HALF
EXTRA = 16
GROUP = 8
VMEM_LIMIT = 20 * 1024 * 1024

XS, YS = 4, 2
CLIP = ("x", "y_lo", "core")
COPY = ("z", "y_hi")
RING = ("y_hi", "z")
ZS, ZY = 8, 2
F32 = jnp.float32
BF16 = jnp.bfloat16

VMEM = pl.BlockSpec(memory_space=pltpu.VMEM)
HBM = pl.BlockSpec(memory_space=pltpu.HBM)


def slot(copy):
    return copy % ZY * ZS + copy // ZY


def copy_of(place):
    return place % ZS * ZY + place // ZS


def in_order(blocks):
    return jnp.concatenate([blocks(slot(copy)) for copy in range(COPIES)], axis=0)


def frame_ids(width):
    row = lax.broadcasted_iota(jnp.int32, (L, width), 0)
    return (copy_of(row // ROWS) * ROWS + row % ROWS).astype(F32)


def head_here():
    return lax.axis_index("z") * ZY + lax.axis_index("y_hi")


def mm(left, right):
    return jnp.dot(left, right, preferred_element_type=F32)


def mm_nt(left, right):
    return lax.dot_general(left, right, (((1,), (1,)), ((), ())), preferred_element_type=F32)


def call(kernel, name, microseconds, out_shape, in_specs, out_specs, scratch=()):
    return pl.pallas_call(
        kernel,
        out_shape=[
            pltpu.HBM(shape, dtype) if spec is HBM else jax.ShapeDtypeStruct(shape, dtype)
            for (shape, dtype), spec in zip(out_shape, out_specs)
        ],
        in_specs=in_specs,
        out_specs=out_specs,
        scratch_shapes=list(scratch),
        compiler_params=pltpu.CompilerParams(vmem_limit_bytes=VMEM_LIMIT),
        cost_estimate=pl.CostEstimate(
            flops=int(microseconds * 1e9), bytes_accessed=1024, transcendentals=0
        ),
        name=name,
    )


def in_hbm(array):
    return pltpu.with_memory_space_constraint(array, pltpu.HBM)


def pack_kernel(
    slots_hbm, frames_hbm, targets_hbm, index_hbm, w_ref,
    sent_ref, index_out, weights_ref, w_buf, frames_ref, targets_ref, index_ref, slots_ref, sems,
):
    head = head_here()
    copies = []
    load_index = pltpu.make_async_copy(index_hbm.at[0], index_ref, sems.at[3])
    load_index.start()
    load_slots = pltpu.make_async_copy(slots_hbm.at[0], slots_ref, sems.at[7])
    load_slots.start()
    load_frames = pltpu.make_async_copy(frames_hbm.at[0], frames_ref, sems.at[4])
    load_frames.start()
    load_targets = pltpu.make_async_copy(targets_hbm.at[0, :, :EARLY], targets_ref, sems.at[6])
    load_targets.start()
    for part in range(3):
        begin = pl.multiple_of(part * D + (head // 2) * BLOCK, BLOCK)
        copies.append(
            pltpu.make_async_copy(w_ref.at[:, pl.ds(begin, BLOCK)], w_buf.at[part], sems.at[part])
        )
        copies[part].start()
    lanes = lax.broadcasted_iota(jnp.int32, (ROWS, KMAX), 1)
    load_index.wait()
    load_slots.wait()
    kept = jnp.where(slots_ref[...] < KMAX, 1.0, 0.0)
    count = jnp.sum(kept, axis=1, keepdims=True)
    index = jnp.broadcast_to(index_ref[...], (ROWS, KMAX))
    index = jnp.where(lanes.astype(F32) < count, index, L).astype(F32).astype(BF16)
    index_out[...] = index
    load_frames.wait()
    load_targets.wait()
    for m in range(COPIES):
        sent_ref[m, :, :D] = frames_ref[...]
        sent_ref[m, :, D : D + KMAX] = index
        sent_ref[m, :, D + KMAX :] = targets_ref[...]
    odd = head % 2 == 1
    for part in range(3):
        copies[part].wait()
    q, k, v = [
        jnp.where(odd, w_buf[part, :, HS:].astype(F32), w_buf[part, :, :HS].astype(F32)) for part in range(3)
    ]
    weights_ref[:HS, :] = jnp.concatenate([q, k], axis=1).astype(BF16)
    weights_ref[HS:QKV, :] = jnp.concatenate([v[:HALF], v[HALF:]], axis=1).astype(BF16)


def pack(slots, frames, targets, index, w_qkv):
    return call(
        pack_kernel,
        "pack",
        1,
        [((COPIES, ROWS, D + KMAX + EARLY), BF16), ((ROWS, KMAX), BF16), ((QKV, BLOCK), BF16)],
        [HBM] * 5,
        [VMEM, VMEM, VMEM],
        [
            pltpu.VMEM((3, HS, BLOCK), BF16),
            pltpu.VMEM((ROWS, D), BF16),
            pltpu.VMEM((ROWS, EARLY), BF16),
            pltpu.VMEM((1, KMAX), jnp.int32),
            pltpu.VMEM((1, L), jnp.int32),
            pltpu.SemaphoreType.DMA((8,)),
        ],
    )(in_hbm(slots), in_hbm(frames), in_hbm(targets), in_hbm(index), in_hbm(w_qkv))


def normalize(got_ref, gain_hbm, gain_ref, sem):
    load = pltpu.make_async_copy(gain_hbm, gain_ref, sem)
    load.start()
    values = got_ref[:, :D].astype(F32)
    center = values - jnp.mean(values, axis=1, keepdims=True)
    spread = jnp.mean(center * center, axis=1, keepdims=True)
    load.wait()
    return (center * lax.rsqrt(spread + NORM_EPSILON) * gain_ref[...]).astype(BF16)


def forward_kernel(
    got_ref, w_ref, gain_hbm, targets_ref, out_ref, probs_out, pick_out, qkv_out,
    probs_ref, pick_ref, qkv_ref, wqk_ref, wv_ref, gain_ref, sems,
):
    for m in range(COPIES):
        for a in range((D - EARLY) // BLOCK):
            lanes = slice(EARLY + a * BLOCK, EARLY + (a + 1) * BLOCK)
            out_ref[m, HS + a * ROWS : HS + (a + 1) * ROWS, :] = targets_ref[0, :, lanes]
    normed = normalize(got_ref, gain_hbm, gain_ref, sems.at[3 * COPIES // GROUP])
    x = lax.axis_index("x")
    for c in range(CLIPS):
        block = w_ref[c % 2, lax.rem(x + XS - c // (2 * YS), XS), c // 2 % YS]
        wqk_ref[c * HS : (c + 1) * HS, :] = block[:HS]
        wv_ref[c * HS : c * HS + HALF, :] = block[HS:, :HS]
        wv_ref[c * HS + HALF : (c + 1) * HS, :] = block[HS:, HS:]
    qk = mm(normed, wqk_ref[...]).astype(BF16).astype(F32)
    v = mm(normed, wv_ref[...]).astype(BF16).astype(F32)
    qk_t = qk.T
    qkv_t = jnp.concatenate([qk_t[:HS] * SCORE_SCALE, qk_t[HS:], v.T], axis=0).astype(BF16)
    rows = frame_ids(KMAX)
    first = lax.broadcasted_iota(jnp.int32, (EXTRA, KMAX), 0) == 0
    one_row = jnp.where(first, 1.0, 0.0).astype(BF16)
    saves = []

    def save(here, there):
        saves.append(pltpu.make_async_copy(here, there, sems.at[len(saves)]))
        saves[-1].start()

    for begin in range(0, COPIES, GROUP):
        group = range(begin, begin + GROUP)
        index = [got_ref[m * ROWS : (m + 1) * ROWS, D : D + KMAX].astype(F32)[:1] for m in group]
        pick = [jnp.where(rows == i, 1.0, 0.0).astype(BF16) for i in index]
        for m, p in zip(group, pick):
            pick_ref[:, m * KMAX : (m + 1) * KMAX] = p
        qkv = [mm(qkv_t, p).astype(BF16) for p in pick]
        for m, a in zip(group, qkv):
            qkv_ref[m] = a
        part = pl.ds(begin, GROUP)
        lanes = pl.ds(begin * KMAX, GROUP * KMAX)
        save(pick_ref.at[:, lanes], pick_out.at[:, lanes])
        save(qkv_ref.at[part], qkv_out.at[part])
        bias = [jnp.where(first & (i > L - 0.5), MASKED_SCORE, 0.0).astype(BF16) for i in index]
        queries = [jnp.concatenate([a[:HS], one_row], axis=0) for a in qkv]
        keys = [jnp.concatenate([a[HS : 2 * HS], e], axis=0).T for a, e in zip(qkv, bias)]
        scores = [mm(k, q) for k, q in zip(keys, queries)]
        raised = [jnp.exp(a - jnp.max(a, axis=0, keepdims=True)) for a in scores]
        probs = [a * (1.0 / jnp.sum(a, axis=0, keepdims=True)) for a in raised]
        for m, p in zip(group, probs):
            probs_ref[m] = p
        ctx = [mm(a[2 * HS :], p.astype(BF16)) for a, p in zip(qkv, probs)]
        for m, a in zip(group, ctx):
            out_ref[m, :HS, :] = a.astype(BF16)
        save(probs_ref.at[part], probs_out.at[part])
    for copy in saves:
        copy.wait()


def forward(got, weights, gain, targets):
    return call(
        forward_kernel,
        "forward",
        0.1,
        [
            ((COPIES, HS + LATE, KMAX), BF16),
            ((COPIES, KMAX, KMAX), F32),
            ((L, QALL), BF16),
            ((COPIES, 3 * HS, KMAX), BF16),
        ],
        [VMEM, VMEM, HBM, VMEM],
        [VMEM, HBM, HBM, HBM],
        [
            pltpu.VMEM((COPIES, KMAX, KMAX), F32),
            pltpu.VMEM((L, QALL), BF16),
            pltpu.VMEM((COPIES, 3 * HS, KMAX), BF16),
            pltpu.VMEM((D, 2 * HS), BF16),
            pltpu.VMEM((D, HS), BF16),
            pltpu.VMEM((1, D), F32),
            pltpu.SemaphoreType.DMA((3 * COPIES // GROUP + 1,)),
        ],
    )(got, weights, in_hbm(gain), targets)


def prepare_kernel(got_ref, gain_hbm, out_ref, buf, gain_ref, sems):
    buf[...] = normalize(got_ref, gain_hbm, gain_ref, sems.at[1]).T
    save = pltpu.make_async_copy(buf, out_ref, sems.at[0])
    save.start()
    save.wait()


def prepare(got, gain):
    return call(
        prepare_kernel,
        "prepare",
        2,
        [((D, L), BF16)],
        [VMEM, HBM],
        [HBM],
        [pltpu.VMEM((D, L), BF16), pltpu.VMEM((1, D), F32), pltpu.SemaphoreType.DMA((2,))],
    )(got, in_hbm(gain))[0]


def decoder_kernel(
    recv_ref, got_ref, index_ref, embed_ref, taps_ref, *refs
):
    w_refs = refs[: 2 * XS]
    encoded_out, dctx_out, ctx_out, denc_out, share_out = refs[2 * XS : 2 * XS + 5]
    encoded_ref, dctx_ref, ctx_ref, denc_ref, share_ref, field_ref, error_ref, dfilled_ref, sems = refs[2 * XS + 5 :]
    chunks = D // LANES
    core, x, y = lax.axis_index("core"), lax.axis_index("x"), lax.axis_index("y_lo")
    parts = []
    for s in range(XS):
        chip = YS * lax.rem(x + XS - s, XS)
        slots = [
            side * ZS + chip + lax.rem(y + YS - t, YS) for side in (core, 1 - core) for t in range(YS)
        ]
        weights = jnp.concatenate(
            [w_refs[s][...].reshape(YS * HS, D), w_refs[XS + s][...].reshape(YS * HS, D)], axis=0
        )
        parts.append((slots, weights))
    rows = lax.broadcasted_iota(jnp.int32, (L, KMAX), 0).astype(F32)
    hit = jnp.where(rows == index_ref[...].astype(F32)[:1], 1.0, 0.0)
    masked = 1.0 - jnp.sum(hit, axis=1, keepdims=True)
    place = hit.astype(BF16)
    hit = hit.T
    live = jnp.sum(hit, axis=1, keepdims=True) > 0.5
    pick = hit.astype(BF16)
    gather = jnp.where(frame_ids(KMAX) == index_ref[...].astype(F32)[:1], 1.0, 0.0).T.astype(BF16)
    ctx_ref[...] = recv_ref[:, :HS, :]
    saves = [
        pltpu.make_async_copy(here, there, sems.at[at])
        for at, (here, there) in enumerate(
            ((ctx_ref, ctx_out), (denc_ref, denc_out), (share_ref, share_out), (encoded_ref, encoded_out))
        )
    ]
    saves[0].start()
    ctx = [
        jnp.concatenate([ctx_ref[at] for at in slots], axis=0).T for slots, weights in parts
    ]
    for i in range(CLIPS // 2):
        share_ref[i, :HS, :] = ctx_ref[(1 - core) * ZS + i]
    reach = KW // 2
    blocks = D // BLOCK
    for ref in (field_ref, error_ref):
        ref[:PAD] = jnp.zeros((PAD, D), F32)
        ref[PAD + L :] = jnp.zeros((PAD, D), F32)
    inside = slice(PAD, PAD + L)
    columns = [slice(c * LANES, (c + 1) * LANES) for c in range(chunks)]
    inputs = [mm(gather, got_ref[:, lanes]) for lanes in columns]
    per = LANES // BLOCK
    mixed = inputs
    for left, (slots, weights) in zip(ctx, parts):
        mixed = [m + mm(left, weights[:, lanes]) for m, lanes in zip(mixed, columns)]
    encoded = [jnp.where(live, m, 0.0).astype(BF16) for m in mixed]
    for lanes, e in zip(columns, encoded):
        encoded_ref[:, lanes] = e
    saves[3].start()
    for lanes, e in zip(columns, encoded):
        field_ref[inside, lanes] = mm(place, e) + masked * embed_ref[:, lanes].astype(F32)
    for a in range(blocks):
        lanes = slice(a * BLOCK, (a + 1) * BLOCK)
        predicted = taps_ref[:1, lanes] * field_ref[PAD - reach : PAD - reach + L, lanes]
        for t in range(1, KW):
            begin = PAD - reach + t
            predicted = predicted + taps_ref[t : t + 1, lanes] * field_ref[begin : begin + L, lanes]
        if (a + 1) * BLOCK <= EARLY:
            begin = D + KMAX + a * BLOCK
            wanted = in_order(lambda p: got_ref[p * ROWS : (p + 1) * ROWS, begin : begin + BLOCK])
        else:
            begin = HS + (a * BLOCK - EARLY) // BLOCK * ROWS
            wanted = in_order(lambda p: recv_ref[p, begin : begin + ROWS, :])
        error_ref[inside, lanes] = masked * (predicted - wanted.astype(F32)) * LOSS_SCALE
    for a in range(blocks):
        lanes = slice(a * BLOCK, (a + 1) * BLOCK)
        dfilled = taps_ref[:1, lanes] * error_ref[PAD + reach : PAD + reach + L, lanes]
        for t in range(1, KW):
            begin = PAD + reach - t
            dfilled = dfilled + taps_ref[t : t + 1, lanes] * error_ref[begin : begin + L, lanes]
        dfilled_ref[:, lanes] = dfilled.astype(BF16)
    denc = [mm(pick, dfilled_ref[:, lanes]).astype(BF16) for lanes in columns]
    for c in range(chunks):
        denc_ref[:, columns[c]] = denc[c]
        for i in range(per):
            share_ref[c * per + i, HS:, :] = denc[c][:, i * BLOCK : (i + 1) * BLOCK]
    saves[1].start()
    saves[2].start()
    denc = denc_ref[...]
    for slots, weights in parts:
        dctx = mm_nt(weights, denc).astype(BF16)
        for r, at in enumerate(slots):
            dctx_ref[at] = dctx[r * HS : (r + 1) * HS]
            saves.append(pltpu.make_async_copy(dctx_ref.at[at], dctx_out.at[at], sems.at[len(saves)]))
            saves[-1].start()
    for save in saves:
        save.wait()


def decoder(recv, got, w_out, index, embed, taps):
    return call(
        decoder_kernel,
        "decoder",
        5,
        [
            ((KMAX, D), BF16),
            ((H, HS, KMAX), BF16),
            ((H, HS, KMAX), BF16),
            ((KMAX, D), BF16),
            ((CLIPS // 2, HS + KMAX, KMAX), BF16),
        ],
        [VMEM] * (5 + 2 * XS),
        [HBM] * 5,
        [
            pltpu.VMEM((KMAX, D), BF16),
            pltpu.VMEM((H, HS, KMAX), BF16),
            pltpu.VMEM((H, HS, KMAX), BF16),
            pltpu.VMEM((KMAX, D), BF16),
            pltpu.VMEM((CLIPS // 2, HS + KMAX, KMAX), BF16),
            pltpu.VMEM((L + 2 * PAD, D), F32),
            pltpu.VMEM((L + 2 * PAD, D), F32),
            pltpu.VMEM((L, D), BF16),
            pltpu.SemaphoreType.DMA((4 + H,)),
        ],
    )(recv, got, index, embed, taps, *w_out)


def out_grad_kernel(ctx_ref, denc_ref, share_ref, *refs):
    outs, both_ref = refs[:XS], refs[XS]
    core, x, y = lax.axis_index("core"), lax.axis_index("x"), lax.axis_index("y_lo")
    for a in range(D // BLOCK):
        lanes = slice(a * BLOCK, (a + 1) * BLOCK)
        both_ref[:KMAX, lanes] = denc_ref[:, lanes]
        both_ref[KMAX:, lanes] = share_ref[a, HS:, :]
    for r in range(XS):
        for s in range(YS):
            chip = YS * lax.rem(x + r, XS) + lax.rem(y + s, YS)
            left = jnp.concatenate([ctx_ref[core * ZS + chip], share_ref[chip, :HS, :]], axis=1)
            block = mm(left, both_ref[...])
            upper, lower = block[:HALF], block[HALF:]
            for a in range(D // BLOCK):
                lanes = slice(a * BLOCK, (a + 1) * BLOCK)
                first, second = upper[:, lanes], lower[:, lanes]
                even = jnp.concatenate([first[:, :HS], second[:, :HS]], axis=1)
                odd = jnp.concatenate([first[:, HS:], second[:, HS:]], axis=1)
                outs[r][s, slot(2 * a)] = even.astype(BF16)
                outs[r][s, slot(2 * a + 1)] = odd.astype(BF16)


def out_grad(ctx, denc, share):
    return call(
        out_grad_kernel,
        "out_grad",
        1,
        [((YS, COPIES, HALF, BLOCK), BF16)] * XS,
        [VMEM] * 3,
        [VMEM] * XS,
        [pltpu.VMEM((2 * KMAX, D), BF16)],
    )(ctx, denc, share)


def backward_kernel(
    dctx_ref, probs_ref, pick_hbm, qkv_ref, normed_hbm, out_ref, pick_ref, normed_ref, dqkv_ref, sems
):
    loads = []
    for at, (there, here) in enumerate(((pick_hbm, pick_ref), (normed_hbm, normed_ref))):
        loads.append(pltpu.make_async_copy(there, here, sems.at[at]))
        loads[at].start()
    for begin in range(0, COPIES, GROUP):
        group = range(begin, begin + GROUP)
        dctx = [dctx_ref[m] for m in group]
        qkv = [qkv_ref[m] for m in group]
        probs = [probs_ref[m] for m in group]
        dprobs = [mm(a[2 * HS :].T, d) for a, d in zip(qkv, dctx)]
        along = [jnp.sum(p * d, axis=0, keepdims=True) for p, d in zip(probs, dprobs)]
        dscores = [(p * (d - a)).astype(BF16) for p, d, a in zip(probs, dprobs, along)]
        dvalue = [mm(p.astype(BF16), d.T) for p, d in zip(probs, dctx)]
        dkey = [mm(d, a[:HS].T) for d, a in zip(dscores, qkv)]
        dquery = [(mm(a[HS : 2 * HS], d) * SCORE_SCALE).T for a, d in zip(qkv, dscores)]
        for m, q, k, v in zip(group, dquery, dkey, dvalue):
            dqkv = jnp.concatenate([q, k, v], axis=1)
            dqkv_ref[m * KMAX : (m + 1) * KMAX, :] = dqkv.astype(BF16)
    loads[0].wait()
    loads[1].wait()
    total = mm(pick_ref[...], dqkv_ref[...]).astype(BF16)
    grad = mm(normed_ref[...], total).astype(BF16)
    for c in range(CLIPS):
        block = grad[c * HS : (c + 1) * HS]
        out_ref[c, :HS, :] = block[:, : 2 * HS]
        out_ref[c, HS:, :HS] = block[:HALF, 2 * HS :]
        out_ref[c, HS:, HS:] = block[HALF:, 2 * HS :]


def backward(dctx, probs, pick, qkv, normed):
    return call(
        backward_kernel,
        "backward",
        5,
        [((CLIPS, HS + HALF, BLOCK), BF16)],
        [VMEM, VMEM, HBM, VMEM, HBM],
        [VMEM],
        [
            pltpu.VMEM((L, QALL), BF16),
            pltpu.VMEM((D, L), BF16),
            pltpu.VMEM((QALL, 3 * HS), BF16),
            pltpu.SemaphoreType.DMA((2,)),
        ],
    )(dctx, probs, in_hbm(pick), qkv, in_hbm(normed))[0]


def collect_kernel(terms_ref, mine_ref, other_ref, out_ref):
    head = head_here()
    out_ref[:, :HALF, :] = (mine_ref[...].astype(F32) + other_ref[...].astype(F32)).astype(BF16)
    out_ref[:, HALF:, :] = jnp.zeros((COPIES, HALF, BLOCK), BF16)
    term = jnp.sum(terms_ref[...].astype(F32), axis=0)
    upper, lower = term[:HALF], term[HALF:HS]
    query = jnp.concatenate([upper[:, :HS], lower[:, :HS]], axis=1)
    key = jnp.concatenate([upper[:, HS:], lower[:, HS:]], axis=1)
    for part, piece in enumerate((query, key, term[HS:])):
        out_ref[slot((part * H + head) // 3), HALF:, :] = piece.astype(BF16)


def collect(terms, mine, other):
    return call(
        collect_kernel,
        "collect",
        1,
        [((COPIES, HS, BLOCK), BF16)],
        [VMEM] * 3,
        [VMEM],
    )(terms, mine, other)[0]


def emit_kernel(source_hbm, out_ref, buf, sem):
    load = pltpu.make_async_copy(source_hbm, buf, sem)
    load.start()
    load.wait()
    out_ref[...] = buf[...]


def emit(encoded):
    return call(
        emit_kernel,
        "emit",
        5,
        [((KMAX, D), BF16)],
        [HBM],
        [VMEM],
        [pltpu.VMEM((KMAX, D), BF16), pltpu.SemaphoreType.DMA(())],
    )(in_hbm(encoded))[0]


def finish_kernel(last_ref, qkv_ref, out_ref):
    total = jnp.sum(last_ref[:, :HALF, :].astype(F32), axis=0)
    out_ref[:HALF, :] = total[:, :HS]
    out_ref[HALF:, :] = total[:, HS:]
    for i in range(3):
        block = last_ref[slot(lax.rem(3 * head_here() + i, COPIES)), HALF:, :].astype(F32)
        qkv_ref[:HALF, i * HS : (i + 1) * HS] = block[:, :HS]
        qkv_ref[HALF:, i * HS : (i + 1) * HS] = block[:, HS:]


def finish(last):
    return call(
        finish_kernel,
        "finish",
        1,
        [((HS, 3 * HS), F32), ((HS, HS), F32)],
        [VMEM],
        [VMEM] * 2,
    )(last)


def swap(array, axes):
    return lax.all_to_all(array, axes, 0, 0, tiled=True)


def total(*parts):
    result = parts[0].astype(F32)
    for part in parts[1:]:
        result = result + part.astype(F32)
    return result.astype(BF16)


def per_device(
    frames,
    targets,
    kept_index,
    kept_count,
    fill_slot,
    norm_gain,
    w_qkv,
    w_out,
    mask_embed,
    dec_kernel,
):
    gain = norm_gain[None, :]
    sent, index, weights = pack(fill_slot, frames, targets, kept_index, w_qkv)
    got = swap(sent, RING).reshape(L, D + KMAX + EARLY)
    pair = lax.all_gather(weights, "y_lo", axis=0)
    around = [pair] + [
        lax.ppermute(pair, "x", [(i, (i + r) % XS) for i in range(XS)]) for r in range(1, XS)
    ]
    weights = lax.all_gather(jnp.stack(around), "core", axis=0)
    beyond, pair = lax.optimization_barrier((w_out, pair))
    beyond = lax.ppermute(beyond, "y_lo", [(0, 1), (1, 0)])
    weights, beyond = lax.optimization_barrier((weights, beyond))

    sent, probs, pick, qkv = forward(got, weights, gain, targets)
    normed = prepare(got, gain)
    recv = swap(sent, RING)
    near, sent = lax.optimization_barrier((jnp.stack([w_out, beyond]), sent))
    w_out = [near]
    for r in range(1, XS):
        w_out.append(lax.ppermute(near, "x", [(i, (i + r) % XS) for i in range(XS)]))
    w_out += [lax.ppermute(part, "core", [(0, 1), (1, 0)]) for part in w_out]
    encoded, dctx, ctx, denc, share = decoder(
        recv, got, w_out, index, mask_embed[None, :], dec_kernel
    )
    dctx = swap(dctx, RING)

    share = lax.ppermute(share, "core", [(0, 1), (1, 0)])
    parts = list(out_grad(ctx, denc, share))
    for r in range(1, XS):
        parts[r] = lax.ppermute(parts[r], "x", [(i, (i + r) % XS) for i in range(XS)])
    other = total(*[part[1] for part in parts])
    other, parts = lax.optimization_barrier((other, parts))
    mine = total(*[part[0] for part in parts])
    other = lax.ppermute(other, "y_lo", [(0, 1), (1, 0)])

    terms = swap(backward(dctx, probs, pick, qkv, normed), CLIP)
    grad_qkv, grad_out = finish(swap(collect(terms, mine, other), RING))
    return (emit(encoded)[None, None], grad_qkv, grad_out)


def solution(mesh):
    fine = Mesh(mesh.devices.reshape(XS, YS, 2, 8, 2), ("x", "y_lo", "core", "z", "y_hi"))
    in_specs = (
        P(CLIP, COPY, None),
        P(CLIP, COPY, None),
        P(CLIP, COPY, None),
        P(CLIP, COPY),
        P(CLIP, COPY, None),
        P(),
        P(CLIP, None),
        P(CLIP, None),
        P(),
        P(),
    )
    out_specs = (P(CLIP, COPY, None, None), P(CLIP, COPY), P(CLIP, COPY))
    return jax.shard_map(
        per_device, mesh=fine, in_specs=in_specs, out_specs=out_specs, check_vma=False
    )
```

```python
import jax
import jax.numpy as jnp
from jax import lax
from jax.experimental import pallas as pl
from jax.experimental.pallas import tpu as pltpu
from jax.sharding import Mesh
from jax.sharding import PartitionSpec as P


D = 1024
H = 16
HS = 64
HALF = HS // 2
L = 256
KMAX = 128
KW = 7
CLIPS = 16
COPIES = 16
QALL = COPIES * KMAX
NORM_EPSILON = 1e-05
MASKED_SCORE = -1e30
SCORE_SCALE = HS**-0.5
ROWS = L // COPIES
LOSS_SCALE = (KMAX * CLIPS * COPIES) ** -0.5
PAD = 8
LANES = 256
BLOCK = 128
EARLY = D // 8
LATE = (D - EARLY) // BLOCK * ROWS
QKV = HS + HALF
EXTRA = 16
GROUP = 8
VMEM_LIMIT = 20 * 1024 * 1024

XS, YS = 4, 2
CLIP = ("x", "y_lo", "core")
COPY = ("z", "y_hi")
RING = ("y_hi", "z")
ZS, ZY = 8, 2
F32 = jnp.float32
BF16 = jnp.bfloat16

VMEM = pl.BlockSpec(memory_space=pltpu.VMEM)
HBM = pl.BlockSpec(memory_space=pltpu.HBM)


def slot(copy):
    return copy % ZY * ZS + copy // ZY


def copy_of(place):
    return place % ZS * ZY + place // ZS


def in_order(blocks):
    return jnp.concatenate([blocks(slot(copy)) for copy in range(COPIES)], axis=0)


def frame_ids(width):
    row = lax.broadcasted_iota(jnp.int32, (L, width), 0)
    return (copy_of(row // ROWS) * ROWS + row % ROWS).astype(F32)


def head_here():
    return lax.axis_index("z") * ZY + lax.axis_index("y_hi")


def mm(left, right):
    return jnp.dot(left, right, preferred_element_type=F32)


def mm_nt(left, right):
    return lax.dot_general(left, right, (((1,), (1,)), ((), ())), preferred_element_type=F32)


def call(kernel, name, microseconds, out_shape, in_specs, out_specs, scratch=()):
    return pl.pallas_call(
        kernel,
        out_shape=[
            pltpu.HBM(shape, dtype) if spec is HBM else jax.ShapeDtypeStruct(shape, dtype)
            for (shape, dtype), spec in zip(out_shape, out_specs)
        ],
        in_specs=in_specs,
        out_specs=out_specs,
        scratch_shapes=list(scratch),
        compiler_params=pltpu.CompilerParams(vmem_limit_bytes=VMEM_LIMIT),
        cost_estimate=pl.CostEstimate(
            flops=int(microseconds * 1e9), bytes_accessed=1024, transcendentals=0
        ),
        name=name,
    )


def in_hbm(array):
    return pltpu.with_memory_space_constraint(array, pltpu.HBM)


def pack_kernel(
    slots_hbm, frames_hbm, targets_hbm, index_hbm, w_ref,
    sent_ref, index_out, weights_ref, w_buf, frames_ref, targets_ref, index_ref, slots_ref, sems,
):
    head = head_here()
    copies = []
    load_index = pltpu.make_async_copy(index_hbm.at[0], index_ref, sems.at[3])
    load_index.start()
    load_slots = pltpu.make_async_copy(slots_hbm.at[0], slots_ref, sems.at[7])
    load_slots.start()
    load_frames = pltpu.make_async_copy(frames_hbm.at[0], frames_ref, sems.at[4])
    load_frames.start()
    load_targets = pltpu.make_async_copy(targets_hbm.at[0, :, :EARLY], targets_ref, sems.at[6])
    load_targets.start()
    for part in range(3):
        begin = pl.multiple_of(part * D + (head // 2) * BLOCK, BLOCK)
        copies.append(
            pltpu.make_async_copy(w_ref.at[:, pl.ds(begin, BLOCK)], w_buf.at[part], sems.at[part])
        )
        copies[part].start()
    lanes = lax.broadcasted_iota(jnp.int32, (ROWS, KMAX), 1)
    load_index.wait()
    load_slots.wait()
    kept = jnp.where(slots_ref[...] < KMAX, 1.0, 0.0)
    count = jnp.sum(kept, axis=1, keepdims=True)
    index = jnp.broadcast_to(index_ref[...], (ROWS, KMAX))
    index = jnp.where(lanes.astype(F32) < count, index, L).astype(F32).astype(BF16)
    index_out[...] = index
    load_frames.wait()
    load_targets.wait()
    for m in range(COPIES):
        sent_ref[m, :, :D] = frames_ref[...]
        sent_ref[m, :, D : D + KMAX] = index
        sent_ref[m, :, D + KMAX :] = targets_ref[...]
    odd = head % 2 == 1
    for part in range(3):
        copies[part].wait()
    q, k, v = [
        jnp.where(odd, w_buf[part, :, HS:].astype(F32), w_buf[part, :, :HS].astype(F32)) for part in range(3)
    ]
    weights_ref[:HS, :] = jnp.concatenate([q, k], axis=1).astype(BF16)
    weights_ref[HS:QKV, :] = jnp.concatenate([v[:HALF], v[HALF:]], axis=1).astype(BF16)


def pack(slots, frames, targets, index, w_qkv):
    return call(
        pack_kernel,
        "pack",
        1,
        [((COPIES, ROWS, D + KMAX + EARLY), BF16), ((ROWS, KMAX), BF16), ((QKV, BLOCK), BF16)],
        [HBM] * 5,
        [VMEM, VMEM, VMEM],
        [
            pltpu.VMEM((3, HS, BLOCK), BF16),
            pltpu.VMEM((ROWS, D), BF16),
            pltpu.VMEM((ROWS, EARLY), BF16),
            pltpu.VMEM((1, KMAX), jnp.int32),
            pltpu.VMEM((1, L), jnp.int32),
            pltpu.SemaphoreType.DMA((8,)),
        ],
    )(in_hbm(slots), in_hbm(frames), in_hbm(targets), in_hbm(index), in_hbm(w_qkv))


def normalize(got_ref, gain_hbm, gain_ref, sem):
    load = pltpu.make_async_copy(gain_hbm, gain_ref, sem)
    load.start()
    values = got_ref[:, :D].astype(F32)
    center = values - jnp.mean(values, axis=1, keepdims=True)
    spread = jnp.mean(center * center, axis=1, keepdims=True)
    load.wait()
    return (center * lax.rsqrt(spread + NORM_EPSILON) * gain_ref[...]).astype(BF16)


def forward_kernel(
    got_ref, w_ref, gain_hbm, targets_ref, out_ref, probs_out, pick_out, qkv_out,
    probs_ref, pick_ref, qkv_ref, wqk_ref, wv_ref, gain_ref, sems,
):
    for m in range(COPIES):
        for a in range((D - EARLY) // BLOCK):
            lanes = slice(EARLY + a * BLOCK, EARLY + (a + 1) * BLOCK)
            out_ref[m, HS + a * ROWS : HS + (a + 1) * ROWS, :] = targets_ref[0, :, lanes]
    normed = normalize(got_ref, gain_hbm, gain_ref, sems.at[3 * COPIES // GROUP])
    x = lax.axis_index("x")
    for c in range(CLIPS):
        block = w_ref[c % 2, lax.rem(x + XS - c // (2 * YS), XS), c // 2 % YS]
        wqk_ref[c * HS : (c + 1) * HS, :] = block[:HS]
        wv_ref[c * HS : c * HS + HALF, :] = block[HS:, :HS]
        wv_ref[c * HS + HALF : (c + 1) * HS, :] = block[HS:, HS:]
    qk = mm(normed, wqk_ref[...]).astype(BF16).astype(F32)
    v = mm(normed, wv_ref[...]).astype(BF16).astype(F32)
    qk_t = qk.T
    qkv_t = jnp.concatenate([qk_t[:HS] * SCORE_SCALE, qk_t[HS:], v.T], axis=0).astype(BF16)
    rows = frame_ids(KMAX)
    first = lax.broadcasted_iota(jnp.int32, (EXTRA, KMAX), 0) == 0
    one_row = jnp.where(first, 1.0, 0.0).astype(BF16)
    saves = []

    def save(here, there):
        saves.append(pltpu.make_async_copy(here, there, sems.at[len(saves)]))
        saves[-1].start()

    for begin in range(0, COPIES, GROUP):
        group = range(begin, begin + GROUP)
        index = [got_ref[m * ROWS : (m + 1) * ROWS, D : D + KMAX].astype(F32)[:1] for m in group]
        pick = [jnp.where(rows == i, 1.0, 0.0).astype(BF16) for i in index]
        for m, p in zip(group, pick):
            pick_ref[:, m * KMAX : (m + 1) * KMAX] = p
        qkv = [mm(qkv_t, p).astype(BF16) for p in pick]
        for m, a in zip(group, qkv):
            qkv_ref[m] = a
        part = pl.ds(begin, GROUP)
        lanes = pl.ds(begin * KMAX, GROUP * KMAX)
        save(pick_ref.at[:, lanes], pick_out.at[:, lanes])
        save(qkv_ref.at[part], qkv_out.at[part])
        bias = [jnp.where(first & (i > L - 0.5), MASKED_SCORE, 0.0).astype(BF16) for i in index]
        queries = [jnp.concatenate([a[:HS], one_row], axis=0) for a in qkv]
        keys = [jnp.concatenate([a[HS : 2 * HS], e], axis=0).T for a, e in zip(qkv, bias)]
        scores = [mm(k, q) for k, q in zip(keys, queries)]
        raised = [jnp.exp(a - jnp.max(a, axis=0, keepdims=True)) for a in scores]
        probs = [a * (1.0 / jnp.sum(a, axis=0, keepdims=True)) for a in raised]
        for m, p in zip(group, probs):
            probs_ref[m] = p
        ctx = [mm(a[2 * HS :], p.astype(BF16)) for a, p in zip(qkv, probs)]
        for m, a in zip(group, ctx):
            out_ref[m, :HS, :] = a.astype(BF16)
        save(probs_ref.at[part], probs_out.at[part])
    for copy in saves:
        copy.wait()


def forward(got, weights, gain, targets):
    return call(
        forward_kernel,
        "forward",
        0.1,
        [
            ((COPIES, HS + LATE, KMAX), BF16),
            ((COPIES, KMAX, KMAX), F32),
            ((L, QALL), BF16),
            ((COPIES, 3 * HS, KMAX), BF16),
        ],
        [VMEM, VMEM, HBM, VMEM],
        [VMEM, HBM, HBM, HBM],
        [
            pltpu.VMEM((COPIES, KMAX, KMAX), F32),
            pltpu.VMEM((L, QALL), BF16),
            pltpu.VMEM((COPIES, 3 * HS, KMAX), BF16),
            pltpu.VMEM((D, 2 * HS), BF16),
            pltpu.VMEM((D, HS), BF16),
            pltpu.VMEM((1, D), F32),
            pltpu.SemaphoreType.DMA((3 * COPIES // GROUP + 1,)),
        ],
    )(got, weights, in_hbm(gain), targets)


def prepare_kernel(got_ref, gain_hbm, out_ref, buf, gain_ref, sems):
    buf[...] = normalize(got_ref, gain_hbm, gain_ref, sems.at[1]).T
    save = pltpu.make_async_copy(buf, out_ref, sems.at[0])
    save.start()
    save.wait()


def prepare(got, gain):
    return call(
        prepare_kernel,
        "prepare",
        2,
        [((D, L), BF16)],
        [VMEM, HBM],
        [HBM],
        [pltpu.VMEM((D, L), BF16), pltpu.VMEM((1, D), F32), pltpu.SemaphoreType.DMA((2,))],
    )(got, in_hbm(gain))[0]


def decoder_kernel(
    recv_ref, got_ref, index_ref, embed_ref, taps_ref, *refs
):
    w_refs = refs[: 2 * XS]
    encoded_out, dctx_out, ctx_out, denc_out, share_out = refs[2 * XS : 2 * XS + 5]
    encoded_ref, dctx_ref, ctx_ref, denc_ref, share_ref, field_ref, error_ref, dfilled_ref, sems = refs[2 * XS + 5 :]
    chunks = D // LANES
    core, x, y = lax.axis_index("core"), lax.axis_index("x"), lax.axis_index("y_lo")
    parts = []
    for s in range(XS):
        chip = YS * lax.rem(x + XS - s, XS)
        slots = [
            side * ZS + chip + lax.rem(y + YS - t, YS) for side in (core, 1 - core) for t in range(YS)
        ]
        weights = jnp.concatenate(
            [w_refs[s][...].reshape(YS * HS, D), w_refs[XS + s][...].reshape(YS * HS, D)], axis=0
        )
        parts.append((slots, weights))
    rows = lax.broadcasted_iota(jnp.int32, (L, KMAX), 0).astype(F32)
    hit = jnp.where(rows == index_ref[...].astype(F32)[:1], 1.0, 0.0)
    masked = 1.0 - jnp.sum(hit, axis=1, keepdims=True)
    place = hit.astype(BF16)
    hit = hit.T
    live = jnp.sum(hit, axis=1, keepdims=True) > 0.5
    pick = hit.astype(BF16)
    gather = jnp.where(frame_ids(KMAX) == index_ref[...].astype(F32)[:1], 1.0, 0.0).T.astype(BF16)
    ctx_ref[...] = recv_ref[:, :HS, :]
    saves = [
        pltpu.make_async_copy(here, there, sems.at[at])
        for at, (here, there) in enumerate(
            ((ctx_ref, ctx_out), (denc_ref, denc_out), (share_ref, share_out), (encoded_ref, encoded_out))
        )
    ]
    saves[0].start()
    ctx = [
        jnp.concatenate([ctx_ref[at] for at in slots], axis=0).T for slots, weights in parts
    ]
    for i in range(CLIPS // 2):
        share_ref[i, :HS, :] = ctx_ref[(1 - core) * ZS + i]
    reach = KW // 2
    blocks = D // BLOCK
    for ref in (field_ref, error_ref):
        ref[:PAD] = jnp.zeros((PAD, D), F32)
        ref[PAD + L :] = jnp.zeros((PAD, D), F32)
    inside = slice(PAD, PAD + L)
    columns = [slice(c * LANES, (c + 1) * LANES) for c in range(chunks)]
    inputs = [mm(gather, got_ref[:, lanes]) for lanes in columns]
    per = LANES // BLOCK
    mixed = inputs
    for left, (slots, weights) in zip(ctx, parts):
        mixed = [m + mm(left, weights[:, lanes]) for m, lanes in zip(mixed, columns)]
    encoded = [jnp.where(live, m, 0.0).astype(BF16) for m in mixed]
    for lanes, e in zip(columns, encoded):
        encoded_ref[:, lanes] = e
    saves[3].start()
    for lanes, e in zip(columns, encoded):
        field_ref[inside, lanes] = mm(place, e) + masked * embed_ref[:, lanes].astype(F32)
    for a in range(blocks):
        lanes = slice(a * BLOCK, (a + 1) * BLOCK)
        predicted = taps_ref[:1, lanes] * field_ref[PAD - reach : PAD - reach + L, lanes]
        for t in range(1, KW):
            begin = PAD - reach + t
            predicted = predicted + taps_ref[t : t + 1, lanes] * field_ref[begin : begin + L, lanes]
        if (a + 1) * BLOCK <= EARLY:
            begin = D + KMAX + a * BLOCK
            wanted = in_order(lambda p: got_ref[p * ROWS : (p + 1) * ROWS, begin : begin + BLOCK])
        else:
            begin = HS + (a * BLOCK - EARLY) // BLOCK * ROWS
            wanted = in_order(lambda p: recv_ref[p, begin : begin + ROWS, :])
        error_ref[inside, lanes] = masked * (predicted - wanted.astype(F32)) * LOSS_SCALE
    for a in range(blocks):
        lanes = slice(a * BLOCK, (a + 1) * BLOCK)
        dfilled = taps_ref[:1, lanes] * error_ref[PAD + reach : PAD + reach + L, lanes]
        for t in range(1, KW):
            begin = PAD + reach - t
            dfilled = dfilled + taps_ref[t : t + 1, lanes] * error_ref[begin : begin + L, lanes]
        dfilled_ref[:, lanes] = dfilled.astype(BF16)
    denc = [mm(pick, dfilled_ref[:, lanes]).astype(BF16) for lanes in columns]
    for c in range(chunks):
        denc_ref[:, columns[c]] = denc[c]
        for i in range(per):
            share_ref[c * per + i, HS:, :] = denc[c][:, i * BLOCK : (i + 1) * BLOCK]
    saves[1].start()
    saves[2].start()
    denc = denc_ref[...]
    for slots, weights in parts:
        dctx = mm_nt(weights, denc).astype(BF16)
        for r, at in enumerate(slots):
            dctx_ref[at] = dctx[r * HS : (r + 1) * HS]
            saves.append(pltpu.make_async_copy(dctx_ref.at[at], dctx_out.at[at], sems.at[len(saves)]))
            saves[-1].start()
    for save in saves:
        save.wait()


def decoder(recv, got, w_out, index, embed, taps):
    return call(
        decoder_kernel,
        "decoder",
        5,
        [
            ((KMAX, D), BF16),
            ((H, HS, KMAX), BF16),
            ((H, HS, KMAX), BF16),
            ((KMAX, D), BF16),
            ((CLIPS // 2, HS + KMAX, KMAX), BF16),
        ],
        [VMEM] * (5 + 2 * XS),
        [HBM] * 5,
        [
            pltpu.VMEM((KMAX, D), BF16),
            pltpu.VMEM((H, HS, KMAX), BF16),
            pltpu.VMEM((H, HS, KMAX), BF16),
            pltpu.VMEM((KMAX, D), BF16),
            pltpu.VMEM((CLIPS // 2, HS + KMAX, KMAX), BF16),
            pltpu.VMEM((L + 2 * PAD, D), F32),
            pltpu.VMEM((L + 2 * PAD, D), F32),
            pltpu.VMEM((L, D), BF16),
            pltpu.SemaphoreType.DMA((4 + H,)),
        ],
    )(recv, got, index, embed, taps, *w_out)


def out_grad_kernel(ctx_ref, denc_ref, share_ref, *refs):
    outs, both_ref = refs[:XS], refs[XS]
    core, x, y = lax.axis_index("core"), lax.axis_index("x"), lax.axis_index("y_lo")
    for a in range(D // BLOCK):
        lanes = slice(a * BLOCK, (a + 1) * BLOCK)
        both_ref[:KMAX, lanes] = denc_ref[:, lanes]
        both_ref[KMAX:, lanes] = share_ref[a, HS:, :]
    for r in range(XS):
        for s in range(YS):
            chip = YS * lax.rem(x + r, XS) + lax.rem(y + s, YS)
            left = jnp.concatenate([ctx_ref[core * ZS + chip], share_ref[chip, :HS, :]], axis=1)
            block = mm(left, both_ref[...])
            upper, lower = block[:HALF], block[HALF:]
            for a in range(D // BLOCK):
                lanes = slice(a * BLOCK, (a + 1) * BLOCK)
                first, second = upper[:, lanes], lower[:, lanes]
                even = jnp.concatenate([first[:, :HS], second[:, :HS]], axis=1)
                odd = jnp.concatenate([first[:, HS:], second[:, HS:]], axis=1)
                outs[r][s, slot(2 * a)] = even.astype(BF16)
                outs[r][s, slot(2 * a + 1)] = odd.astype(BF16)


def out_grad(ctx, denc, share):
    return call(
        out_grad_kernel,
        "out_grad",
        1,
        [((YS, COPIES, HALF, BLOCK), BF16)] * XS,
        [VMEM] * 3,
        [VMEM] * XS,
        [pltpu.VMEM((2 * KMAX, D), BF16)],
    )(ctx, denc, share)


def backward_kernel(
    dctx_ref, probs_ref, pick_hbm, qkv_ref, normed_hbm, out_ref, pick_ref, normed_ref, dqkv_ref, sems
):
    loads = []
    for at, (there, here) in enumerate(((pick_hbm, pick_ref), (normed_hbm, normed_ref))):
        loads.append(pltpu.make_async_copy(there, here, sems.at[at]))
        loads[at].start()
    for begin in range(0, COPIES, GROUP):
        group = range(begin, begin + GROUP)
        dctx = [dctx_ref[m] for m in group]
        qkv = [qkv_ref[m] for m in group]
        probs = [probs_ref[m] for m in group]
        dprobs = [mm(a[2 * HS :].T, d) for a, d in zip(qkv, dctx)]
        along = [jnp.sum(p * d, axis=0, keepdims=True) for p, d in zip(probs, dprobs)]
        dscores = [(p * (d - a)).astype(BF16) for p, d, a in zip(probs, dprobs, along)]
        dvalue = [mm(p.astype(BF16), d.T) for p, d in zip(probs, dctx)]
        dkey = [mm(d, a[:HS].T) for d, a in zip(dscores, qkv)]
        dquery = [(mm(a[HS : 2 * HS], d) * SCORE_SCALE).T for a, d in zip(qkv, dscores)]
        for m, q, k, v in zip(group, dquery, dkey, dvalue):
            dqkv = jnp.concatenate([q, k, v], axis=1)
            dqkv_ref[m * KMAX : (m + 1) * KMAX, :] = dqkv.astype(BF16)
    loads[0].wait()
    loads[1].wait()
    total = mm(pick_ref[...], dqkv_ref[...]).astype(BF16)
    grad = mm(normed_ref[...], total).astype(BF16)
    for c in range(CLIPS):
        block = grad[c * HS : (c + 1) * HS]
        out_ref[c, :HS, :] = block[:, : 2 * HS]
        out_ref[c, HS:, :HS] = block[:HALF, 2 * HS :]
        out_ref[c, HS:, HS:] = block[HALF:, 2 * HS :]


def backward(dctx, probs, pick, qkv, normed):
    return call(
        backward_kernel,
        "backward",
        5,
        [((CLIPS, HS + HALF, BLOCK), BF16)],
        [VMEM, VMEM, HBM, VMEM, HBM],
        [VMEM],
        [
            pltpu.VMEM((L, QALL), BF16),
            pltpu.VMEM((D, L), BF16),
            pltpu.VMEM((QALL, 3 * HS), BF16),
            pltpu.SemaphoreType.DMA((2,)),
        ],
    )(dctx, probs, in_hbm(pick), qkv, in_hbm(normed))[0]


def collect_kernel(terms_ref, mine_ref, other_ref, out_ref):
    head = head_here()
    out_ref[:, :HALF, :] = (mine_ref[...].astype(F32) + other_ref[...].astype(F32)).astype(BF16)
    out_ref[:, HALF:, :] = jnp.zeros((COPIES, HALF, BLOCK), BF16)
    term = jnp.sum(terms_ref[...].astype(F32), axis=0)
    upper, lower = term[:HALF], term[HALF:HS]
    query = jnp.concatenate([upper[:, :HS], lower[:, :HS]], axis=1)
    key = jnp.concatenate([upper[:, HS:], lower[:, HS:]], axis=1)
    for part, piece in enumerate((query, key, term[HS:])):
        out_ref[slot((part * H + head) // 3), HALF:, :] = piece.astype(BF16)


def collect(terms, mine, other):
    return call(
        collect_kernel,
        "collect",
        1,
        [((COPIES, HS, BLOCK), BF16)],
        [VMEM] * 3,
        [VMEM],
    )(terms, mine, other)[0]


def emit_kernel(source_hbm, out_ref, buf, sem):
    load = pltpu.make_async_copy(source_hbm, buf, sem)
    load.start()
    load.wait()
    out_ref[...] = buf[...]


def emit(encoded):
    return call(
        emit_kernel,
        "emit",
        5,
        [((KMAX, D), BF16)],
        [HBM],
        [VMEM],
        [pltpu.VMEM((KMAX, D), BF16), pltpu.SemaphoreType.DMA(())],
    )(in_hbm(encoded))[0]


def finish_kernel(last_ref, qkv_ref, out_ref):
    total = jnp.sum(last_ref[:, :HALF, :].astype(F32), axis=0)
    out_ref[:HALF, :] = total[:, :HS]
    out_ref[HALF:, :] = total[:, HS:]
    for i in range(3):
        block = last_ref[slot(lax.rem(3 * head_here() + i, COPIES)), HALF:, :].astype(F32)
        qkv_ref[:HALF, i * HS : (i + 1) * HS] = block[:, :HS]
        qkv_ref[HALF:, i * HS : (i + 1) * HS] = block[:, HS:]


def finish(last):
    return call(
        finish_kernel,
        "finish",
        1,
        [((HS, 3 * HS), F32), ((HS, HS), F32)],
        [VMEM],
        [VMEM] * 2,
    )(last)


def swap(array, axes):
    return lax.all_to_all(array, axes, 0, 0, tiled=True)


def total(*parts):
    result = parts[0].astype(F32)
    for part in parts[1:]:
        result = result + part.astype(F32)
    return result.astype(BF16)


def per_device(
    frames,
    targets,
    kept_index,
    kept_count,
    fill_slot,
    norm_gain,
    w_qkv,
    w_out,
    mask_embed,
    dec_kernel,
):
    gain = norm_gain[None, :]
    sent, index, weights = pack(fill_slot, frames, targets, kept_index, w_qkv)
    got = swap(sent, RING).reshape(L, D + KMAX + EARLY)
    pair = lax.all_gather(weights, "y_lo", axis=0)
    around = [pair] + [
        lax.ppermute(pair, "x", [(i, (i + r) % XS) for i in range(XS)]) for r in range(1, XS)
    ]
    weights = lax.all_gather(jnp.stack(around), "core", axis=0)
    beyond, pair = lax.optimization_barrier((w_out, pair))
    beyond = lax.ppermute(beyond, "y_lo", [(0, 1), (1, 0)])
    weights, beyond = lax.optimization_barrier((weights, beyond))

    sent, probs, pick, qkv = forward(got, weights, gain, targets)
    normed = prepare(got, gain)
    recv = swap(sent, RING)
    near, sent = lax.optimization_barrier((jnp.stack([w_out, beyond]), sent))
    w_out = [near]
    for r in range(1, XS):
        w_out.append(lax.ppermute(near, "x", [(i, (i + r) % XS) for i in range(XS)]))
    w_out += [lax.ppermute(part, "core", [(0, 1), (1, 0)]) for part in w_out]
    encoded, dctx, ctx, denc, share = decoder(
        recv, got, w_out, index, mask_embed[None, :], dec_kernel
    )
    dctx = swap(dctx, RING)

    share = lax.ppermute(share, "core", [(0, 1), (1, 0)])
    parts = list(out_grad(ctx, denc, share))
    for r in range(1, XS):
        parts[r] = lax.ppermute(parts[r], "x", [(i, (i + r) % XS) for i in range(XS)])
    other = total(*[part[1] for part in parts])
    other, parts = lax.optimization_barrier((other, parts))
    mine = total(*[part[0] for part in parts])
    other = lax.ppermute(other, "y_lo", [(0, 1), (1, 0)])

    terms = swap(backward(dctx, probs, pick, qkv, normed), CLIP)
    grad_qkv, grad_out = finish(swap(collect(terms, mine, other), RING))
    return (emit(encoded)[None, None], grad_qkv, grad_out)


def solution(mesh):
    fine = Mesh(mesh.devices.reshape(XS, YS, 2, 8, 2), ("x", "y_lo", "core", "z", "y_hi"))
    in_specs = (
        P(CLIP, COPY, None),
        P(CLIP, COPY, None),
        P(CLIP, COPY, None),
        P(CLIP, COPY),
        P(CLIP, COPY, None),
        P(),
        P(CLIP, None),
        P(CLIP, None),
        P(),
        P(),
    )
    out_specs = (P(CLIP, COPY, None, None), P(CLIP, COPY), P(CLIP, COPY))
    return jax.shard_map(
        per_device, mesh=fine, in_specs=in_specs, out_specs=out_specs, check_vma=False
    )
```
